512 devices in a mesh: turb: 32 (over y, z_lo, core), age: 16 (over x, z_hi).
Axes of the slice: x: 4, y: 4, z: 16 (z_hi: 4, z_lo: 4; z = z_hi * 4 + z_lo), core: 2. Of those that a mesh axis runs over, the one named last changes fastest.
Arguments:
- positions: float32 [3, 192, 32768], P(None, 'turb', 'age'), may hold values from -6 to 6
- circulation: float32 [192, 32768], P('turb', 'age'), may hold values from -6 to 6
- send_lists: int32 [32, 16, 32, 6], P('turb', 'age'), may hold values from 0 to 95
- reader_slots: int32 [32, 16, 96, 8], P('turb', 'age'), may hold values from 0 to 191
- source_counts: int32 [32, 16, 96], P('turb', 'age'), may hold values from 1 to 8, as said below
- near_blocks: int32 [32, 16, 96, 4], P('turb', 'age'), may hold values from 0 to 95
Outputs:
- velocity: float32 [3, 192, 32768], P(None, 'turb', 'age')
- moved: float32 [3, 192, 32768], P(None, 'turb', 'age')
The draws below stay inside these ranges and needn't reach their ends.
Inputs may be any that keep to these rules, and one draw needn't show every extreme that they name: `source_counts`: the number of remote sources listed for a reader tile; entries of reader_slots at or past it are unused.
All inputs are finite; a program needn't handle non-finite values.
Results may differ from the reference program's by a relative error of at most 0.0003.
Values sent between devices are 32-bit elements; how exact they have to be, the bound alone decides.
No kernel may reach another device: no remote copies, remote signals or barrier semaphores. Data moves between devices by JAX's collectives and lax.ppermute only.
A program may use at most 64 MiB of HBM per device.

```python
import jax
import jax.numpy as jnp
from jax import lax

SPAN = 64
BLADES = 3
TURB_DEV = 2
AGE_DEV = 32
CAP = 6
KMAX = 8
NEAR = 4
ROWS = 192
AGES = 512
BLOCKS_DEV = 96
SLOTS = 192
N_TURB = 32
N_AGE = 16


def draw_source_counts(key, part):
    first_key, second_key = jax.random.split(jax.random.fold_in(key, 7))
    level = jax.random.randint(first_key, (N_TURB, N_AGE, 1), 1, KMAX + 1)
    level = level.at[0, 0, 0].set(KMAX)
    raw = jax.random.randint(second_key, (N_TURB, N_AGE, BLOCKS_DEV), 0, 1 << 20)
    counts = raw % level + 1
    counts = counts.at[:, :, 0].set(level[:, :, 0])
    return counts.astype(jnp.int32)


def touch_ends(values, own_key, least, top_value):
    place = [jax.random.randint(jax.random.fold_in(own_key, axis), (), 0, length) for axis, length in enumerate(values.shape)]
    longest = values.shape.index(max(values.shape))
    neighbour = place[:longest] + [(place[longest] + 1) % values.shape[longest]] + place[longest + 1:]
    return values.at[tuple(place)].set(least).at[tuple(neighbour)].set(top_value)


def shard_levels(key, extent, cuts, least, top_value):
    loudness = 1.0
    for dim, shards_of in cuts:
        steps = jax.random.uniform(jax.random.fold_in(jax.random.fold_in(key, 6), dim), (shards_of,), jnp.float32, least / len(cuts), top_value / len(cuts))
        loudness = loudness * jnp.repeat(jnp.exp(steps), extent[dim] // shards_of).reshape((-1,) + (1,) * (len(extent) - 1 - dim))
    return loudness


def scatter_about(key, dims, deviation, most, cuts=(), kind=jnp.bfloat16):
    values = jax.random.normal(key, dims, jnp.float32) * deviation
    if len(cuts) > 0:
        values = shard_levels(key, dims, cuts, -0.22, 0.18) * values
    return jnp.clip(values, min=-most, max=most).astype(kind)


def setup_inputs(seed: int = 0) -> dict:
    keys = jax.random.split(jax.random.key(seed), 7)
    positions = scatter_about(keys[0], (3, ROWS, AGES * SPAN), 1.0, 6.0, ((1, 32), (2, 16)), jnp.float32)
    circulation = scatter_about(keys[1], (ROWS, AGES * SPAN), 1.0, 6.0, ((0, 32), (1, 16)), jnp.float32)
    send_lists = touch_ends(jax.random.randint(keys[2], (N_TURB, N_AGE, N_TURB, CAP), 0, BLOCKS_DEV), jax.random.fold_in(keys[2], 1), 0, BLOCKS_DEV - 1).astype(jnp.int32)
    reader_slots = touch_ends(jax.random.randint(keys[3], (N_TURB, N_AGE, BLOCKS_DEV, KMAX), 0, SLOTS), jax.random.fold_in(keys[3], 1), 0, SLOTS - 1).astype(jnp.int32)
    source_counts = draw_source_counts(jax.random.fold_in(keys[6], 71), 0)
    near_blocks = touch_ends(jax.random.randint(keys[5], (N_TURB, N_AGE, BLOCKS_DEV, NEAR), 0, BLOCKS_DEV), jax.random.fold_in(keys[5], 1), 0, BLOCKS_DEV - 1).astype(jnp.int32)
    return {"positions": positions, "circulation": circulation, "send_lists": send_lists, "reader_slots": reader_slots, "source_counts": source_counts, "near_blocks": near_blocks}


time_step = 0.1
core_square = 0.25
inflow_speed = 1.0
inv_four_pi = 0.07957747154594767

def induce(points, sources):
    apart_x = points[:, 0, :, None] - sources[:, 0, None, :]
    apart_y = points[:, 1, :, None] - sources[:, 1, None, :]
    apart_z = points[:, 2, :, None] - sources[:, 2, None, :]
    square = apart_x * apart_x + apart_y * apart_y + apart_z * apart_z + core_square
    weight = inv_four_pi * lax.rsqrt(square) / square
    strength_x = sources[:, 3, None, :]
    strength_y = sources[:, 4, None, :]
    strength_z = sources[:, 5, None, :]
    cross_x = strength_y * apart_z - strength_z * apart_y
    cross_y = strength_z * apart_x - strength_x * apart_z
    cross_z = strength_x * apart_y - strength_y * apart_x
    return jnp.stack([lax.optimization_barrier(jnp.sum(cross_x * weight, axis=2)), lax.optimization_barrier(jnp.sum(cross_y * weight, axis=2)), lax.optimization_barrier(jnp.sum(cross_z * weight, axis=2))], axis=1)

def blocks_of(field, comps):
    shaped = field.reshape(comps, N_TURB, TURB_DEV * BLADES, N_AGE, AGE_DEV // 2, 2 * SPAN)
    return shaped.transpose(1, 3, 2, 4, 0, 5).reshape(N_TURB, N_AGE, BLOCKS_DEV, comps, 2 * SPAN)

def reference(positions, circulation, send_lists, reader_slots, source_counts, near_blocks):
    grid = positions.reshape(3, ROWS, AGES, SPAN)
    following = jnp.concatenate([grid[:, :, 1:], grid[:, :, -1:]], axis=2)
    segment = (following - grid).reshape(3, ROWS, AGES * SPAN)
    middle = positions + 0.5 * segment
    strength = circulation[None] * segment
    sources = blocks_of(jnp.concatenate([middle, strength], axis=0), 6)
    readers = blocks_of(positions, 3)
    peers = jnp.arange(N_TURB, dtype=jnp.int32)[:, None]

    def device(flat):
        turb_index = flat // N_AGE
        age_index = flat % N_AGE
        chosen = send_lists[:, age_index, turb_index, :]
        column = sources[:, age_index]
        received = column[peers, chosen].reshape(SLOTS, 6, 2 * SPAN)
        points = readers[turb_index, age_index]
        slots = reader_slots[turb_index, age_index]
        counts = source_counts[turb_index, age_index]
        nearby = near_blocks[turb_index, age_index]
        local = sources[turb_index, age_index]
        total = jnp.zeros((BLOCKS_DEV, 3, 2 * SPAN), jnp.float32)
        for index in range(KMAX):
            term = induce(points, received[slots[:, index]])
            total = total + jnp.where((index < counts)[:, None, None], term, 0.0)
        for index in range(NEAR):
            total = total + induce(points, local[nearby[:, index]])
        return total
    blocks = lax.map(device, jnp.arange(N_TURB * N_AGE, dtype=jnp.int32))
    shaped = blocks.reshape(N_TURB, N_AGE, TURB_DEV * BLADES, AGE_DEV // 2, 3, 2 * SPAN)
    velocity = shaped.transpose(4, 0, 2, 1, 3, 5).reshape(3, ROWS, AGES * SPAN)
    inflow = jnp.array([inflow_speed, 0.0, 0.0], jnp.float32)[:, None, None]
    moved = positions + time_step * (velocity + inflow)
    return (velocity, moved)
```

```python
import functools

import jax
import jax.numpy as jnp
from jax import lax
from jax.experimental import pallas as pl
from jax.experimental.pallas import tpu as pltpu
from jax.sharding import PartitionSpec as P

SPAN = 64
TILE = 128
time_step = 0.1
core_square = 0.25
inflow_speed = 1.0
inv_four_pi = 0.07957747154594767
GROUP = 8
DEPTH = 32
F32 = jnp.float32
BF16 = jnp.bfloat16


def split3(value):
    first = value.astype(BF16).astype(F32)
    rest = value - first
    second = rest.astype(BF16).astype(F32)
    third = (rest - second).astype(BF16).astype(F32)
    return first, second, third


def lattice(pos_ref, circ_ref, next_ref, last_ref):
    ends = last_ref[0] == 1
    middles, strengths = [], []
    for comp in range(3):
        here = pos_ref[comp]
        beyond = jnp.where(ends, here[:, -SPAN:], next_ref[comp])
        segment = jnp.concatenate([here[:, SPAN:], beyond], axis=1) - here
        middles.append(here + 0.5 * segment)
        strengths.append(circ_ref[...] * segment)
    return middles, strengths


def source_rows(middle, strength):
    near_rows = []
    for comp in range(3):
        m1, m2, m3 = split3(-2.0 * middle[comp])
        near_rows += [m1, m2, m1, m2, m3, m1]
    square = middle[0] * middle[0] + middle[1] * middle[1] + middle[2] * middle[2] + core_square
    near_rows += [jnp.ones_like(square)] * 3 + list(split3(square))
    w = [inv_four_pi * s for s in strength]
    u = [
        w[1] * middle[2] - w[2] * middle[1],
        w[2] * middle[0] - w[0] * middle[2],
        w[0] * middle[1] - w[1] * middle[0],
    ]
    parts = [split3(v) for v in w + u]
    strength_rows = []
    for half in (parts[:3], parts[3:]):
        for level in range(3):
            strength_rows += [half[comp][level] for comp in range(3)]
    return near_rows, strength_rows


def target_rows(point):
    rows = []
    for comp in range(3):
        x1, x2, x3 = split3(point[comp])
        rows += [x1, x1, x2, x2, x1, x3]
    square = point[0] * point[0] + point[1] * point[1] + point[2] * point[2]
    rows += list(split3(square)) + [jnp.ones_like(square)] * 3
    return rows


def send_kernel(rows, halves, peers, cap, pos_ref, circ_ref, next_ref, last_ref, list_ref, out_ref, stage):
    middles, strengths = lattice(pos_ref, circ_ref, next_ref, last_ref)
    for comp, field in enumerate(middles + strengths):
        for half in range(halves):
            stage[pl.ds(half * 8 + comp, rows, halves * 8), :] = field[:, half * TILE : (half + 1) * TILE]

    def fill(peer, _):
        for c in range(cap):
            block = list_ref[peer * cap + c]
            data = stage[pl.ds(pl.multiple_of(block * 8, 8), 8), :]
            out_ref[peer, c * 6 : c * 6 + 6, :] = data[:6]
        return 0

    lax.fori_loop(0, peers, fill, 0)


def interact(count, item, tt, ss, ww, acc, dsc, ksc):
    def distances(step):
        for u in range(GROUP):
            target, source = item(step * GROUP + u)
            dsc[u] = lax.dot_general(
                tt[jnp.minimum(target, tt.shape[0] - 1)], ss[source], (((1,), (0,)), ((), ())), preferred_element_type=F32
            )

    def kernels():
        for u in range(GROUP):
            inverse = lax.rsqrt(dsc[u])
            weight = inverse * inverse * inverse
            high = weight.astype(BF16)
            ksc[u, :, :TILE] = high
            ksc[u, :, TILE:] = (weight - high.astype(F32)).astype(BF16)

    def gather(step):
        for u in range(0, GROUP, 2):
            t0, s0 = item(step * GROUP + u)
            t1, s1 = item(step * GROUP + u + 1)
            left = jnp.concatenate([ww[s0], ww[s1]], axis=0)
            left = jnp.concatenate([left, left], axis=1)
            right = ksc[u : u + 2].reshape(2 * TILE, 2 * TILE)
            both = lax.dot_general(left, right, (((1,), (1,)), ((), ())), preferred_element_type=F32)
            r0 = pl.ds(pl.multiple_of(t0 * DEPTH, DEPTH), DEPTH)
            acc[r0, :] = acc[r0, :] + both[:DEPTH, :TILE]
            r1 = pl.ds(pl.multiple_of(t1 * DEPTH, DEPTH), DEPTH)
            acc[r1, :] = acc[r1, :] + both[DEPTH:, TILE:]

    acc[...] = jnp.zeros_like(acc)
    distances(0)
    kernels()
    distances(1)

    def step(index, _):
        gather(index)
        kernels()
        distances(index + 2)
        return 0

    lax.fori_loop(0, count, step, 0)


def near_kernel(
    rows, halves, near, kmax,
    pos_ref, circ_ref, next_ref, last_ref, near_ref, slot_ref, count_ref,
    tt_ref, acc_ref, item_ref, total_ref,
    ss, ww, stage, dsc, ksc,
):
    tiles = rows * halves
    middles, strengths = lattice(pos_ref, circ_ref, next_ref, last_ref)
    points = [pos_ref[comp] for comp in range(3)]

    def lay(fields, start):
        for half in range(halves):
            cut = slice(half * TILE, (half + 1) * TILE)
            for r, field in enumerate(fields):
                stage[pl.ds(half * DEPTH + start + r, rows, halves * DEPTH), :] = field[:, cut]

    stage[...] = jnp.zeros_like(stage)
    near_rows, strength_rows = source_rows(middles, strengths)

    def pack_to(dest):
        def pack(b, _):
            dest[b] = stage[pl.ds(pl.multiple_of(b * DEPTH, DEPTH), DEPTH), :].astype(BF16)
            return 0

        lax.fori_loop(0, tiles, pack, 0, unroll=4)

    lay(near_rows, 0)
    pack_to(ss)
    lay(target_rows(points), 0)

    def turn(b, _):
        tt_ref[b] = stage[pl.ds(pl.multiple_of(b * DEPTH, DEPTH), DEPTH), :].T.astype(BF16)
        return 0

    lax.fori_loop(0, tiles, turn, 0, unroll=4)
    stage[...] = jnp.zeros_like(stage)
    lay(strength_rows, 0)
    pack_to(ww)

    def listed(b, at):
        for k in range(kmax):
            item_ref[at + k] = b * 256 + slot_ref[b * kmax + k]
        return at + count_ref[b]

    total = lax.fori_loop(0, tiles, listed, 0)
    for k in range(3 * GROUP):
        item_ref[total + k] = tiles * 256
    total_ref[0] = total

    last = tiles * near - 1

    def item(i):
        i = jnp.minimum(i, last)
        return i // near, near_ref[i]

    interact(tiles * near // GROUP, item, tt_ref, ss, ww, acc_ref, dsc, ksc)


def far_kernel(
    rows, halves, peers, cap, width_rows,
    pos_ref, recv_ref, tt_ref, near_acc, item_ref, total_ref,
    vel_ref, moved_ref,
    ss, ww, stage, acc, dsc, ksc,
):
    stage[...] = jnp.zeros_like(stage)

    def lay(group, _):
        for c in range(cap):
            parts = [
                recv_ref[pl.ds(group * (8 * width_rows) + c * 6 + comp, 8, width_rows), :] for comp in range(6)
            ]
            near_rows, strength_rows = source_rows(parts[:3], parts[3:])
            for r, field in enumerate(near_rows):
                stage[pl.ds(group * (8 * cap * 64) + c * 64 + r, 8, cap * 64), :] = field
            for r, field in enumerate(strength_rows):
                stage[pl.ds(group * (8 * cap * 64) + c * 64 + 32 + r, 8, cap * 64), :] = field
        return 0

    lax.fori_loop(0, peers // 8, lay, 0)

    def pack(b, _):
        ss[b] = stage[pl.ds(pl.multiple_of(b * 64, 64), 32), :].astype(BF16)
        ww[b] = stage[pl.ds(pl.multiple_of(b * 64 + 32, 32), 32), :].astype(BF16)
        return 0

    lax.fori_loop(0, peers * cap, pack, 0, unroll=4)

    def item(i):
        code = item_ref[i]
        return code // 256, code % 256

    total = total_ref[0]
    interact((total + GROUP - 1) // GROUP, item, tt_ref, ss, ww, acc, dsc, ksc)

    for half in range(halves):
        cut = slice(half * TILE, (half + 1) * TILE)
        sums = []
        for first in (0, 9):
            for comp in range(3):
                value = None
                for level in (2, 1, 0):
                    where = pl.ds(half * DEPTH + first + level * 3 + comp, rows, halves * DEPTH)
                    term = acc[where, :] + near_acc[where, :]
                    value = term if value is None else value + term
                sums.append(value)
        point = [pos_ref[comp, :, cut] for comp in range(3)]
        for comp in range(3):
            j, k = (comp + 1) % 3, (comp + 2) % 3
            velocity = sums[j] * point[k] - sums[k] * point[j] - sums[3 + comp]
            vel_ref[comp, :, cut] = velocity
            inflow = inflow_speed if comp == 0 else 0.0
            moved_ref[comp, :, cut] = point[comp] + time_step * (velocity + inflow)


def body(positions, circulation, send_lists, reader_slots, source_counts, near_blocks):
    _, rows, width = positions.shape
    halves = width // TILE
    tiles = rows * halves
    peers = lax.axis_size("turb")
    cap = send_lists.shape[-1]
    kmax = reader_slots.shape[-1]
    near = near_blocks.shape[-1]
    vmem = pl.BlockSpec(memory_space=pltpu.VMEM)
    smem = pl.BlockSpec(memory_space=pltpu.SMEM)
    ages = lax.axis_size("age")
    next_row = lax.ppermute(positions[:, :, :SPAN], "age", [(s, s - 1) for s in range(1, ages)])
    last = (lax.axis_index("age") == ages - 1).astype(jnp.int32).reshape(1)
    width_rows = -(-cap * 6 // 8) * 8
    params = pltpu.CompilerParams(vmem_limit_bytes=48 << 20)

    outgoing = pl.pallas_call(
        functools.partial(send_kernel, rows, halves, peers, cap),
        out_shape=jax.ShapeDtypeStruct((peers, width_rows, TILE), F32),
        in_specs=[vmem, vmem, vmem, smem, smem],
        out_specs=vmem,
        scratch_shapes=[pltpu.VMEM((tiles * 8, TILE), F32)],
        compiler_params=params,
    )(positions, circulation, next_row, last, send_lists.reshape(-1))
    incoming = lax.all_to_all(outgoing, "turb", 0, 0, tiled=True).reshape(peers * width_rows, TILE)

    pairs = [pltpu.VMEM((GROUP, TILE, TILE), F32), pltpu.VMEM((GROUP, TILE, 2 * TILE), BF16)]
    turned, near_acc, items, total = pl.pallas_call(
        functools.partial(near_kernel, rows, halves, near, kmax),
        out_shape=(
            jax.ShapeDtypeStruct((tiles, TILE, DEPTH), BF16),
            jax.ShapeDtypeStruct((tiles * DEPTH, TILE), F32),
            jax.ShapeDtypeStruct((tiles * kmax + 4 * GROUP,), jnp.int32),
            jax.ShapeDtypeStruct((1,), jnp.int32),
        ),
        in_specs=[vmem, vmem, vmem, smem, smem, smem, smem],
        out_specs=(vmem, vmem, smem, smem),
        scratch_shapes=[
            pltpu.VMEM((tiles, DEPTH, TILE), BF16),
            pltpu.VMEM((tiles, DEPTH, TILE), BF16),
            pltpu.VMEM((tiles * DEPTH, TILE), F32),
            *pairs,
        ],
        compiler_params=params,
        cost_estimate=pl.CostEstimate(flops=2 * 10**9, bytes_accessed=4 << 20, transcendentals=tiles * near * TILE * TILE),
    )(
        positions, circulation, next_row, last,
        near_blocks.reshape(-1), reader_slots.reshape(-1), source_counts.reshape(-1),
    )
    return pl.pallas_call(
        functools.partial(far_kernel, rows, halves, peers, cap, width_rows),
        out_shape=(
            jax.ShapeDtypeStruct(positions.shape, F32),
            jax.ShapeDtypeStruct(positions.shape, F32),
        ),
        in_specs=[vmem, vmem, vmem, vmem, smem, smem],
        out_specs=(vmem, vmem),
        scratch_shapes=[
            pltpu.VMEM((peers * cap, DEPTH, TILE), BF16),
            pltpu.VMEM((peers * cap, DEPTH, TILE), BF16),
            pltpu.VMEM((peers * cap * 64, TILE), F32),
            pltpu.VMEM(((tiles + 1) * DEPTH, TILE), F32),
            *pairs,
        ],
        compiler_params=params,
    )(positions, incoming, turned, near_acc, items, total)


def solution(mesh):
    in_specs = (
        P(None, "turb", "age"),
        P("turb", "age"),
        P("turb", "age", None, None),
        P("turb", "age", None, None),
        P("turb", "age", None),
        P("turb", "age", None, None),
    )
    out_specs = (P(None, "turb", "age"), P(None, "turb", "age"))
    return jax.shard_map(body, mesh=mesh, in_specs=in_specs, out_specs=out_specs, check_vma=False)
```

```python
import functools

import jax
import jax.numpy as jnp
from jax import lax
from jax.experimental import pallas as pl
from jax.experimental.pallas import tpu as pltpu
from jax.sharding import PartitionSpec as P

SPAN = 64
TILE = 128
time_step = 0.1
core_square = 0.25
inflow_speed = 1.0
inv_four_pi = 0.07957747154594767
GROUP = 8
STEPS = 4
DEPTH = 32
SUMS = 16
F32 = jnp.float32
BF16 = jnp.bfloat16


def split3(value):
    first = value.astype(BF16).astype(F32)
    rest = value - first
    second = rest.astype(BF16).astype(F32)
    third = (rest - second).astype(BF16).astype(F32)
    return first, second, third


def lattice(pos_ref, circ_ref, next_ref, last_ref):
    ends = last_ref[0] == 1
    middles, strengths = [], []
    for comp in range(3):
        here = pos_ref[comp]
        beyond = jnp.where(ends, here[:, -SPAN:], next_ref[comp])
        segment = jnp.concatenate([here[:, SPAN:], beyond], axis=1) - here
        middles.append(here + 0.5 * segment)
        strengths.append(circ_ref[...] * segment)
    return middles, strengths


def source_rows(middle, strength):
    near_rows = []
    for comp in range(3):
        m1, m2, m3 = split3(-2.0 * middle[comp])
        near_rows += [m1, m2, m1, m2, m3, m1]
    square = middle[0] * middle[0] + middle[1] * middle[1] + middle[2] * middle[2] + core_square
    zero = jnp.zeros_like(square)
    near_rows += [jnp.ones_like(square)] * 3 + list(split3(square)) + [zero] * 8
    w1, w2, w = [], [], []
    for comp in range(3):
        first, second, _ = split3(inv_four_pi * strength[comp])
        w1.append(first)
        w2.append(second)
        w.append(first + second)
    u = [
        split3(w[1] * middle[2] - w[2] * middle[1]),
        split3(w[2] * middle[0] - w[0] * middle[2]),
        split3(w[0] * middle[1] - w[1] * middle[0]),
    ]
    strength_rows = w1 + w2 + [u[comp][level] for level in range(3) for comp in range(3)] + [zero]
    return near_rows, strength_rows


def target_rows(point):
    rows = []
    for comp in range(3):
        x1, x2, x3 = split3(point[comp])
        rows += [x1, x1, x2, x2, x1, x3]
    square = point[0] * point[0] + point[1] * point[1] + point[2] * point[2]
    rows += list(split3(square)) + [jnp.ones_like(square)] * 3 + [jnp.zeros_like(square)] * 8
    return rows


def send_kernel(rows, halves, peers, cap, pos_ref, circ_ref, next_ref, last_ref, list_ref, out_ref, stage):
    middles, strengths = lattice(pos_ref, circ_ref, next_ref, last_ref)
    for comp, field in enumerate(middles + strengths):
        for half in range(halves):
            stage[pl.ds(half * 8 + comp, rows, halves * 8), :] = field[:, half * TILE : (half + 1) * TILE]

    def fill(peer, _):
        for c in range(cap):
            block = list_ref[c, 0, peer]
            data = stage[pl.ds(pl.multiple_of(block * 8, 8), 8), :]
            out_ref[peer, c * 6 : c * 6 + 6, :] = data[:6]
        return 0

    lax.fori_loop(0, peers, fill, 0)


def interact(count, item, tt, st, ww, acc, dsc, ksc):
    most = tt.shape[0] - 1

    def distances(step, side):
        for u in range(GROUP):
            target, source = item(step * GROUP + u)
            half = slice((u % 2) * TILE, (u % 2 + 1) * TILE)
            dsc[side, u // 2, :, half] = lax.dot_general(
                st[source], tt[jnp.minimum(target, most)], (((1,), (0,)), ((), ())), preferred_element_type=F32
            )

    def kernels(side):
        for u in range(GROUP // 2):
            inverse = lax.rsqrt(dsc[side, u])
            weight = inverse * inverse * inverse
            high = weight.astype(BF16)
            ksc[side, u, :TILE] = high
            ksc[side, u, TILE:] = (weight - high.astype(F32)).astype(BF16)

    def gather(step, side):
        for u in range(0, GROUP, 2):
            t0, s0 = item(step * GROUP + u)
            t1, s1 = item(step * GROUP + u + 1)
            left = jnp.concatenate([ww[s0], ww[s1]], axis=0)
            left = jnp.concatenate([left, left], axis=1)
            both = lax.dot_general(left, ksc[side, u // 2], (((1,), (0,)), ((), ())), preferred_element_type=F32)
            r0 = pl.ds(pl.multiple_of(t0 * SUMS, SUMS), SUMS)
            acc[r0, :] = acc[r0, :] + both[:SUMS, :TILE]
            r1 = pl.ds(pl.multiple_of(t1 * SUMS, SUMS), SUMS)
            acc[r1, :] = acc[r1, :] + both[SUMS:, TILE:]

    distances(0, 0)
    kernels(0)
    distances(1, 1)

    def turn(index, _):
        for h in range(STEPS):
            step, side = index * STEPS + h, h % 2
            gather(step, side)
            kernels(1 - side)
            distances(step + 2, side)
        return 0

    lax.fori_loop(0, count, turn, 0)


def near_kernel(
    rows, halves, near, kmax,
    pos_ref, circ_ref, next_ref, last_ref, near_ref, slot_ref, count_ref,
    tt_ref, acc_ref, item_ref, total_ref,
    st, ww, stage, dsc, ksc,
):
    tiles = rows * halves
    middles, strengths = lattice(pos_ref, circ_ref, next_ref, last_ref)
    points = [pos_ref[comp] for comp in range(3)]
    deep = 2 * DEPTH + SUMS

    def lay(fields, start):
        for half in range(halves):
            cut = slice(half * TILE, (half + 1) * TILE)
            for r, field in enumerate(fields):
                stage[pl.ds(half * deep + start + r, rows, halves * deep), :] = field[:, cut]

    near_rows, strength_rows = source_rows(middles, strengths)
    lay(near_rows + target_rows(points) + strength_rows, 0)

    def pack(b, _):
        base = pl.multiple_of(b * deep, SUMS)
        st[b] = stage[pl.ds(base, DEPTH), :].T.astype(BF16)
        tt_ref[b] = stage[pl.ds(base + DEPTH, DEPTH), :].astype(BF16)
        ww[b] = stage[pl.ds(base + 2 * DEPTH, SUMS), :].astype(BF16)
        return 0

    lax.fori_loop(0, tiles, pack, 0, unroll=8)

    def listed(b, at):
        for k in range(kmax):
            item_ref[at + k] = b * 256 + slot_ref[k, b]
        return at + count_ref[b]

    total = lax.fori_loop(0, tiles, listed, 0)
    for k in range((STEPS + 2) * GROUP):
        item_ref[total + k] = tiles * 256
    total_ref[0] = total

    last = tiles * near - 1

    def item(i):
        i = jnp.minimum(i, last)
        b = lax.div(i, near)
        return b, near_ref[i - b * near, b]

    acc_ref[...] = jnp.zeros_like(acc_ref)
    interact(tiles * near // (STEPS * GROUP), item, tt_ref, st, ww, acc_ref, dsc, ksc)


def far_kernel(
    rows, halves, peers, cap, width_rows,
    pos_ref, recv_ref, tt_ref, near_acc, item_ref, total_ref,
    vel_ref, moved_ref,
    st, ww, stage, acc, dsc, ksc,
):
    deep = DEPTH + SUMS

    def lay(group, _):
        for c in range(cap):
            parts = [
                recv_ref[pl.ds(group * (8 * width_rows) + c * 6 + comp, 8, width_rows), :] for comp in range(6)
            ]
            near_rows, strength_rows = source_rows(parts[:3], parts[3:])
            for r, field in enumerate(near_rows + strength_rows):
                stage[pl.ds(group * (8 * cap * deep) + c * deep + r, 8, cap * deep), :] = field
        return 0

    lax.fori_loop(0, peers // 8, lay, 0)

    def pack(b, _):
        base = pl.multiple_of(b * deep, SUMS)
        st[b] = stage[pl.ds(base, DEPTH), :].T.astype(BF16)
        ww[b] = stage[pl.ds(base + DEPTH, SUMS), :].astype(BF16)
        return 0

    lax.fori_loop(0, peers * cap, pack, 0, unroll=8)

    def item(i):
        code = item_ref[i]
        return lax.shift_right_logical(code, 8), lax.bitwise_and(code, 255)

    acc[: rows * halves * SUMS, :] = near_acc[...]
    turns = lax.div(total_ref[0] + STEPS * GROUP - 1, STEPS * GROUP)
    interact(turns, item, tt_ref, st, ww, acc, dsc, ksc)

    for half in range(halves):
        cut = slice(half * TILE, (half + 1) * TILE)

        def summed(*lines):
            value = None
            for line in lines:
                term = acc[pl.ds(half * SUMS + line, rows, halves * SUMS), :]
                value = term if value is None else value + term
            return value

        sums = [summed(3 + comp, comp) for comp in range(3)]
        cross = [summed(12 + comp, 9 + comp, 6 + comp) for comp in range(3)]
        point = [pos_ref[comp, :, cut] for comp in range(3)]
        for comp in range(3):
            j, k = (comp + 1) % 3, (comp + 2) % 3
            velocity = sums[j] * point[k] - sums[k] * point[j] - cross[comp]
            vel_ref[comp, :, cut] = velocity
            inflow = inflow_speed if comp == 0 else 0.0
            moved_ref[comp, :, cut] = point[comp] + time_step * (velocity + inflow)


def body(positions, circulation, send_lists, reader_slots, source_counts, near_blocks):
    _, rows, width = positions.shape
    halves = width // TILE
    tiles = rows * halves
    peers = lax.axis_size("turb")
    cap = send_lists.shape[-1]
    kmax = reader_slots.shape[-1]
    near = near_blocks.shape[-1]
    vmem = pl.BlockSpec(memory_space=pltpu.VMEM)
    smem = pl.BlockSpec(memory_space=pltpu.SMEM)
    ages = lax.axis_size("age")
    next_row = lax.ppermute(positions[:, :, :SPAN], "age", [(s, s - 1) for s in range(1, ages)])
    last = (lax.axis_index("age") == ages - 1).astype(jnp.int32).reshape(1)
    width_rows = -(-cap * 6 // 8) * 8
    params = pltpu.CompilerParams(vmem_limit_bytes=48 << 20)

    outgoing = pl.pallas_call(
        functools.partial(send_kernel, rows, halves, peers, cap),
        out_shape=jax.ShapeDtypeStruct((peers, width_rows, TILE), F32),
        in_specs=[vmem, vmem, vmem, smem, smem],
        out_specs=vmem,
        scratch_shapes=[pltpu.VMEM((tiles * 8, TILE), F32)],
        compiler_params=params,
    )(positions, circulation, next_row, last, send_lists[0, 0].T[:, None])
    incoming = lax.all_to_all(outgoing, "turb", 0, 0, tiled=True).reshape(peers * width_rows, TILE)

    pairs = [
        pltpu.VMEM((2, GROUP // 2, TILE, 2 * TILE), F32),
        pltpu.VMEM((2, GROUP // 2, 2 * TILE, 2 * TILE), BF16),
    ]
    targets, near_acc, items, total = pl.pallas_call(
        functools.partial(near_kernel, rows, halves, near, kmax),
        out_shape=(
            jax.ShapeDtypeStruct((tiles, DEPTH, TILE), BF16),
            jax.ShapeDtypeStruct((tiles * SUMS, TILE), F32),
            jax.ShapeDtypeStruct((tiles * kmax + 64,), jnp.int32),
            jax.ShapeDtypeStruct((1,), jnp.int32),
        ),
        in_specs=[vmem, vmem, vmem, smem, smem, smem, smem],
        out_specs=(vmem, vmem, smem, smem),
        scratch_shapes=[
            pltpu.VMEM((tiles, TILE, DEPTH), BF16),
            pltpu.VMEM((tiles, SUMS, TILE), BF16),
            pltpu.VMEM((tiles * (2 * DEPTH + SUMS), TILE), F32),
            *pairs,
        ],
        compiler_params=params,
        cost_estimate=pl.CostEstimate(flops=2 * 10**9, bytes_accessed=4 << 20, transcendentals=tiles * near * TILE * TILE),
    )(positions, circulation, next_row, last, near_blocks[0, 0].T, reader_slots[0, 0].T, source_counts[0, 0])
    return pl.pallas_call(
        functools.partial(far_kernel, rows, halves, peers, cap, width_rows),
        out_shape=(
            jax.ShapeDtypeStruct(positions.shape, F32),
            jax.ShapeDtypeStruct(positions.shape, F32),
        ),
        in_specs=[vmem, vmem, vmem, vmem, smem, smem],
        out_specs=(vmem, vmem),
        scratch_shapes=[
            pltpu.VMEM((peers * cap, TILE, DEPTH), BF16),
            pltpu.VMEM((peers * cap, SUMS, TILE), BF16),
            pltpu.VMEM((peers * cap * (DEPTH + SUMS), TILE), F32),
            pltpu.VMEM(((tiles + 1) * SUMS, TILE), F32),
            *pairs,
        ],
        compiler_params=params,
    )(positions, incoming, targets, near_acc, items, total)


def solution(mesh):
    in_specs = (
        P(None, "turb", "age"),
        P("turb", "age"),
        P("turb", "age", None, None),
        P("turb", "age", None, None),
        P("turb", "age", None),
        P("turb", "age", None, None),
    )
    out_specs = (P(None, "turb", "age"), P(None, "turb", "age"))
    return jax.shard_map(body, mesh=mesh, in_specs=in_specs, out_specs=out_specs, check_vma=False)
```

```python
import functools

import jax
import jax.numpy as jnp
from jax import lax
from jax.experimental import pallas as pl
from jax.experimental.pallas import tpu as pltpu
from jax.sharding import PartitionSpec as P

SPAN = 64
TILE = 128
time_step = 0.1
core_square = 0.25
inflow_speed = 1.0
inv_four_pi = 0.07957747154594767
GROUP = 8
STEPS = 4
DEPTH = 32
SUMS = 16
F32 = jnp.float32
BF16 = jnp.bfloat16


def split3(value):
    first = value.astype(BF16).astype(F32)
    rest = value - first
    second = rest.astype(BF16).astype(F32)
    third = (rest - second).astype(BF16).astype(F32)
    return first, second, third


def source_rows(middle, strength):
    parts = [split3(-2.0 * middle[comp]) for comp in range(3)]
    square = middle[0] * middle[0] + middle[1] * middle[1] + middle[2] * middle[2] + core_square
    squares = split3(square)
    near_rows = [parts[comp][0] for comp in range(3)] + [parts[comp][1] for comp in range(3)]
    near_rows += [squares[0], squares[1]] + [parts[comp][2] for comp in range(3)] + [squares[2]]
    w1, w2, w = [], [], []
    for comp in range(3):
        first, second, _ = split3(inv_four_pi * strength[comp])
        w1.append(first)
        w2.append(second)
        w.append(first + second)
    u = [
        split3(w[1] * middle[2] - w[2] * middle[1]),
        split3(w[2] * middle[0] - w[0] * middle[2]),
        split3(w[0] * middle[1] - w[1] * middle[0]),
    ]
    strength_rows = w1 + w2 + [u[comp][level] for level in range(3) for comp in range(3)]
    return near_rows, strength_rows


def target_rows(point):
    parts = [split3(point[comp]) for comp in range(3)]
    square = point[0] * point[0] + point[1] * point[1] + point[2] * point[2]
    one, zero = jnp.ones_like(square), jnp.zeros_like(square)
    first, second, third = ([parts[comp][level] for comp in range(3)] for level in range(3))
    return (
        first + first + [one, one]
        + second + second + [zero, zero]
        + third + [zero] * 5
        + first + [one] + list(split3(square)) + [zero]
    )


def fixed_rows(blocks, stage):
    line = lax.broadcasted_iota(jnp.int32, (8, TILE), 0)
    ones = jnp.where((line >= 4) & (line < 7), 1.0, 0.0)

    def fill(b, _):
        stage[pl.ds(pl.multiple_of(b * DEPTH + 8, 8), 8), :] = ones
        stage[pl.ds(pl.multiple_of(b * DEPTH + 24, 8), 8), :] = jnp.zeros_like(ones)
        return 0

    lax.fori_loop(0, blocks, fill, 0, unroll=8)


def pack_sources(blocks, stage, st, ww):
    def pack(b, _):
        base = pl.multiple_of(b * DEPTH, DEPTH)
        top = stage[pl.ds(base, 8), :]
        rest = stage[pl.ds(base + 8, 8), :]
        st[b] = jnp.concatenate([top, top, top, rest], axis=0).T.astype(BF16)
        ww[b] = stage[pl.ds(base + 16, SUMS), :].astype(BF16)
        return 0

    lax.fori_loop(0, blocks, pack, 0, unroll=8)


def source_lines(near_rows, strength_rows):
    return list(enumerate(near_rows)) + [(16 + r, row) for r, row in enumerate(strength_rows)]


def first_kernel(
    rows, halves, kmax, pos_ref, circ_ref, slot_ref, count_ref, field_ref, tt_ref, item_ref, total_ref, stage
):
    tiles = rows * halves
    points = [pos_ref[comp] for comp in range(3)]
    for comp in range(3):
        here = points[comp]
        segment = jnp.concatenate([here[:, SPAN:], here[:, -SPAN:]], axis=1) - here
        middle = here + 0.5 * segment
        strength = circ_ref[...] * segment
        for half in range(halves):
            cut = slice(half * TILE, (half + 1) * TILE)
            field_ref[pl.ds(half * 8 + comp, rows, halves * 8), :] = middle[:, cut]
            field_ref[pl.ds(half * 8 + 3 + comp, rows, halves * 8), :] = strength[:, cut]
    for r, field in enumerate(target_rows(points)):
        for half in range(halves):
            stage[pl.ds(half * DEPTH + r, rows, halves * DEPTH), :] = field[:, half * TILE : (half + 1) * TILE]

    def pack(b, _):
        tt_ref[b] = stage[pl.ds(pl.multiple_of(b * DEPTH, DEPTH), DEPTH), :].astype(BF16)
        return 0

    lax.fori_loop(0, tiles, pack, 0, unroll=8)

    def listed(b, at):
        for k in range(kmax):
            item_ref[at + k] = b * 256 + slot_ref[k, b]
        return at + count_ref[b]

    total = lax.fori_loop(0, tiles, listed, 0)
    for k in range((STEPS + 2) * GROUP):
        item_ref[total + k] = tiles * 256
    total_ref[0] = total


def send_kernel(rows, halves, peers, cap, field_ref, pos_ref, circ_ref, next_ref, last_ref, list_ref, out_ref, full_ref):
    full_ref[...] = field_ref[...]

    @pl.when(last_ref[0] == 0)
    def _():
        width = halves * TILE
        circ = circ_ref[:, width - TILE :]
        for comp in range(3):
            here = pos_ref[comp, :, width - TILE :]
            segment = jnp.concatenate([here[:, SPAN:], next_ref[comp]], axis=1) - here
            at = (halves - 1) * 8 + comp
            full_ref[pl.ds(at, rows, halves * 8), :] = here + 0.5 * segment
            full_ref[pl.ds(at + 3, rows, halves * 8), :] = circ * segment

    def fill(peer, _):
        for c in range(cap):
            block = list_ref[c, 0, peer]
            data = full_ref[pl.ds(pl.multiple_of(block * 8, 8), 8), :]
            out_ref[peer, c * 6 : c * 6 + 6, :] = data[:6]
        return 0

    lax.fori_loop(0, peers, fill, 0, unroll=2)


def interact(count, item, tt, st, ww, acc, dsc, ksc):
    most = tt.shape[0] - 1

    def distances(step, side):
        for u in range(GROUP):
            target, source = item(step * GROUP + u)
            half = slice((u % 2) * TILE, (u % 2 + 1) * TILE)
            dsc[side, u // 2, :, half] = lax.dot_general(
                st[source], tt[jnp.minimum(target, most)], (((1,), (0,)), ((), ())), preferred_element_type=F32
            )

    def kernels(side):
        for u in range(GROUP // 2):
            inverse = lax.rsqrt(dsc[side, u])
            weight = inverse * inverse * inverse
            high = weight.astype(BF16)
            ksc[side, u, :TILE] = high
            ksc[side, u, TILE:] = (weight - high.astype(F32)).astype(BF16)

    def gather(step, side):
        for u in range(0, GROUP, 2):
            t0, s0 = item(step * GROUP + u)
            t1, s1 = item(step * GROUP + u + 1)
            left = jnp.concatenate([ww[s0], ww[s1]], axis=0)
            left = jnp.concatenate([left, left], axis=1)
            both = lax.dot_general(left, ksc[side, u // 2], (((1,), (0,)), ((), ())), preferred_element_type=F32)
            r0 = pl.ds(pl.multiple_of(t0 * SUMS, SUMS), SUMS)
            acc[r0, :] = acc[r0, :] + both[:SUMS, :TILE]
            r1 = pl.ds(pl.multiple_of(t1 * SUMS, SUMS), SUMS)
            acc[r1, :] = acc[r1, :] + both[SUMS:, TILE:]

    distances(0, 0)
    kernels(0)
    distances(1, 1)

    def turn(index, _):
        for h in range(STEPS):
            step, side = index * STEPS + h, h % 2
            gather(step, side)
            kernels(1 - side)
            distances(step + 2, side)
        return 0

    lax.fori_loop(0, count, turn, 0)


def near_kernel(rows, halves, near, full_ref, tt_ref, near_ref, acc_ref, st, ww, stage, dsc, ksc):
    tiles = rows * halves
    fixed_rows(tiles, stage)
    for half in range(halves):
        parts = [full_ref[pl.ds(half * 8 + comp, rows, halves * 8), :] for comp in range(6)]
        for r, field in source_lines(*source_rows(parts[:3], parts[3:])):
            stage[pl.ds(half * DEPTH + r, rows, halves * DEPTH), :] = field
    pack_sources(tiles, stage, st, ww)
    last = tiles * near - 1

    def item(i):
        i = jnp.minimum(i, last)
        b = lax.div(i, near)
        return b, near_ref[i - b * near, b]

    acc_ref[...] = jnp.zeros_like(acc_ref)
    interact(tiles * near // (STEPS * GROUP), item, tt_ref, st, ww, acc_ref, dsc, ksc)


def far_kernel(
    rows, halves, peers, cap, width_rows,
    pos_ref, recv_ref, tt_ref, near_acc, item_ref, total_ref,
    vel_ref, moved_ref,
    st, ww, stage, acc, dsc, ksc,
):
    fixed_rows(peers * cap, stage)

    def lay(group, _):
        for c in range(cap):
            parts = [
                recv_ref[pl.ds(group * (8 * width_rows) + c * 6 + comp, 8, width_rows), :] for comp in range(6)
            ]
            for r, field in source_lines(*source_rows(parts[:3], parts[3:])):
                stage[pl.ds(group * (8 * cap * DEPTH) + c * DEPTH + r, 8, cap * DEPTH), :] = field
        return 0

    lax.fori_loop(0, peers // 8, lay, 0)
    pack_sources(peers * cap, stage, st, ww)

    def item(i):
        code = item_ref[i]
        return lax.shift_right_logical(code, 8), lax.bitwise_and(code, 255)

    acc[: rows * halves * SUMS, :] = near_acc[...]
    turns = lax.div(total_ref[0] + STEPS * GROUP - 1, STEPS * GROUP)
    interact(turns, item, tt_ref, st, ww, acc, dsc, ksc)

    for half in range(halves):
        cut = slice(half * TILE, (half + 1) * TILE)

        def summed(*lines):
            value = None
            for line in lines:
                term = acc[pl.ds(half * SUMS + line, rows, halves * SUMS), :]
                value = term if value is None else value + term
            return value

        sums = [summed(3 + comp, comp) for comp in range(3)]
        cross = [summed(12 + comp, 9 + comp, 6 + comp) for comp in range(3)]
        point = [pos_ref[comp, :, cut] for comp in range(3)]
        for comp in range(3):
            j, k = (comp + 1) % 3, (comp + 2) % 3
            velocity = sums[j] * point[k] - sums[k] * point[j] - cross[comp]
            vel_ref[comp, :, cut] = velocity
            inflow = inflow_speed if comp == 0 else 0.0
            moved_ref[comp, :, cut] = point[comp] + time_step * (velocity + inflow)


def body(positions, circulation, send_lists, reader_slots, source_counts, near_blocks):
    _, rows, width = positions.shape
    halves = width // TILE
    tiles = rows * halves
    peers = lax.axis_size("turb")
    cap = send_lists.shape[-1]
    kmax = reader_slots.shape[-1]
    near = near_blocks.shape[-1]
    vmem = pl.BlockSpec(memory_space=pltpu.VMEM)
    smem = pl.BlockSpec(memory_space=pltpu.SMEM)
    ages = lax.axis_size("age")
    next_row = lax.ppermute(positions[:, :, :SPAN], "age", [(s, s - 1) for s in range(1, ages)])
    last = (lax.axis_index("age") == ages - 1).astype(jnp.int32).reshape(1)
    width_rows = -(-cap * 6 // 8) * 8
    params = pltpu.CompilerParams(vmem_limit_bytes=48 << 20)

    fields, targets, items, total = pl.pallas_call(
        functools.partial(first_kernel, rows, halves, kmax),
        out_shape=(
            jax.ShapeDtypeStruct((tiles * 8, TILE), F32),
            jax.ShapeDtypeStruct((tiles, DEPTH, TILE), BF16),
            jax.ShapeDtypeStruct((tiles * kmax + 64,), jnp.int32),
            jax.ShapeDtypeStruct((1,), jnp.int32),
        ),
        in_specs=[vmem, vmem, smem, smem],
        out_specs=(vmem, vmem, smem, smem),
        scratch_shapes=[pltpu.VMEM((tiles * DEPTH, TILE), F32)],
        compiler_params=params,
        cost_estimate=pl.CostEstimate(flops=10**8, bytes_accessed=2 << 20, transcendentals=0),
    )(positions, circulation, reader_slots[0, 0].T, source_counts[0, 0])
    outgoing, full = pl.pallas_call(
        functools.partial(send_kernel, rows, halves, peers, cap),
        out_shape=(
            jax.ShapeDtypeStruct((peers, width_rows, TILE), F32),
            jax.ShapeDtypeStruct((tiles * 8, TILE), F32),
        ),
        in_specs=[vmem, vmem, vmem, vmem, smem, smem],
        out_specs=(vmem, vmem),
        compiler_params=params,
    )(fields, positions, circulation, next_row, last, send_lists[0, 0].T[:, None])
    incoming = lax.all_to_all(outgoing, "turb", 0, 0, tiled=True).reshape(peers * width_rows, TILE)

    pairs = [
        pltpu.VMEM((2, GROUP // 2, TILE, 2 * TILE), F32),
        pltpu.VMEM((2, GROUP // 2, 2 * TILE, 2 * TILE), BF16),
    ]
    near_acc = pl.pallas_call(
        functools.partial(near_kernel, rows, halves, near),
        out_shape=jax.ShapeDtypeStruct((tiles * SUMS, TILE), F32),
        in_specs=[vmem, vmem, smem],
        out_specs=vmem,
        scratch_shapes=[
            pltpu.VMEM((tiles, TILE, DEPTH), BF16),
            pltpu.VMEM((tiles, SUMS, TILE), BF16),
            pltpu.VMEM((tiles * DEPTH, TILE), F32),
            *pairs,
        ],
        compiler_params=params,
        cost_estimate=pl.CostEstimate(flops=2 * 10**9, bytes_accessed=4 << 20, transcendentals=tiles * near * TILE * TILE),
    )(full, targets, near_blocks[0, 0].T)
    return pl.pallas_call(
        functools.partial(far_kernel, rows, halves, peers, cap, width_rows),
        out_shape=(
            jax.ShapeDtypeStruct(positions.shape, F32),
            jax.ShapeDtypeStruct(positions.shape, F32),
        ),
        in_specs=[vmem, vmem, vmem, vmem, smem, smem],
        out_specs=(vmem, vmem),
        scratch_shapes=[
            pltpu.VMEM((peers * cap, TILE, DEPTH), BF16),
            pltpu.VMEM((peers * cap, SUMS, TILE), BF16),
            pltpu.VMEM((peers * cap * DEPTH, TILE), F32),
            pltpu.VMEM(((tiles + 1) * SUMS, TILE), F32),
            *pairs,
        ],
        compiler_params=params,
    )(positions, incoming, targets, near_acc, items, total)


def solution(mesh):
    in_specs = (
        P(None, "turb", "age"),
        P("turb", "age"),
        P("turb", "age", None, None),
        P("turb", "age", None, None),
        P("turb", "age", None),
        P("turb", "age", None, None),
    )
    out_specs = (P(None, "turb", "age"), P(None, "turb", "age"))
    return jax.shard_map(body, mesh=mesh, in_specs=in_specs, out_specs=out_specs, check_vma=False)
```

```python
import functools

import jax
import jax.numpy as jnp
from jax import lax
from jax.experimental import pallas as pl
from jax.experimental.pallas import tpu as pltpu
from jax.sharding import PartitionSpec as P

SPAN = 64
TILE = 128
time_step = 0.1
core_square = 0.25
inflow_speed = 1.0
inv_four_pi = 0.07957747154594767
GROUP = 8
STEPS = 4
DEPTH = 32
SUMS = 16
F32 = jnp.float32
BF16 = jnp.bfloat16


def split3(value):
    first = value.astype(BF16).astype(F32)
    rest = value - first
    second = rest.astype(BF16).astype(F32)
    third = (rest - second).astype(BF16).astype(F32)
    return first, second, third


def source_rows(middle, strength):
    parts = [split3(-2.0 * middle[comp]) for comp in range(3)]
    square = middle[0] * middle[0] + middle[1] * middle[1] + middle[2] * middle[2] + core_square
    squares = split3(square)
    near_rows = [parts[comp][0] for comp in range(3)] + [parts[comp][1] for comp in range(3)]
    near_rows += [squares[0], squares[1]] + [parts[comp][2] for comp in range(3)] + [squares[2]]
    w1, w2, w = [], [], []
    for comp in range(3):
        first, second, _ = split3(inv_four_pi * strength[comp])
        w1.append(first)
        w2.append(second)
        w.append(first + second)
    u = [
        split3(w[1] * middle[2] - w[2] * middle[1]),
        split3(w[2] * middle[0] - w[0] * middle[2]),
        split3(w[0] * middle[1] - w[1] * middle[0]),
    ]
    strength_rows = w1 + w2 + [u[comp][level] for level in range(3) for comp in range(3)]
    return near_rows, strength_rows


def target_rows(point):
    parts = [split3(point[comp]) for comp in range(3)]
    square = point[0] * point[0] + point[1] * point[1] + point[2] * point[2]
    one, zero = jnp.ones_like(square), jnp.zeros_like(square)
    first, second, third = ([parts[comp][level] for comp in range(3)] for level in range(3))
    return (
        first + first + [one, one]
        + second + second + [zero, zero]
        + third + [zero] * 5
        + first + [one] + list(split3(square)) + [zero]
    )


def fixed_rows(blocks, stage):
    line = lax.broadcasted_iota(jnp.int32, (8, TILE), 0)
    ones = jnp.where((line >= 4) & (line < 7), 1.0, 0.0)

    def fill(b, _):
        stage[pl.ds(pl.multiple_of(b * DEPTH + 8, 8), 8), :] = ones
        stage[pl.ds(pl.multiple_of(b * DEPTH + 24, 8), 8), :] = jnp.zeros_like(ones)
        return 0

    lax.fori_loop(0, blocks, fill, 0, unroll=8)


def pack_sources(blocks, stage, st, ww):
    def pack(b, _):
        base = pl.multiple_of(b * DEPTH, DEPTH)
        top = stage[pl.ds(base, 8), :]
        rest = stage[pl.ds(base + 8, 8), :]
        st[b] = jnp.concatenate([top, top, top, rest], axis=0).T.astype(BF16)
        ww[b] = stage[pl.ds(base + 16, SUMS), :].astype(BF16)
        return 0

    lax.fori_loop(0, blocks, pack, 0, unroll=8)


def source_lines(near_rows, strength_rows):
    return list(enumerate(near_rows)) + [(16 + r, row) for r, row in enumerate(strength_rows)]


def send_kernel(
    rows, halves, peers, cap, pos_hbm, circ_hbm, next_ref, last_ref, list_ref, out_ref, full_ref, pos_ref, circ_ref, sems
):
    copies = [
        pltpu.make_async_copy(pos_hbm, pos_ref, sems.at[0]),
        pltpu.make_async_copy(circ_hbm, circ_ref, sems.at[1]),
    ]
    for copy in copies:
        copy.start()
    for copy in copies:
        copy.wait()
    ends = last_ref[0] == 1
    for comp in range(3):
        here = pos_ref[comp]
        beyond = jnp.where(ends, here[:, -SPAN:], next_ref[comp])
        segment = jnp.concatenate([here[:, SPAN:], beyond], axis=1) - here
        middle = here + 0.5 * segment
        strength = circ_ref[...] * segment
        for half in range(halves):
            cut = slice(half * TILE, (half + 1) * TILE)
            full_ref[pl.ds(half * 8 + comp, rows, halves * 8), :] = middle[:, cut]
            full_ref[pl.ds(half * 8 + 3 + comp, rows, halves * 8), :] = strength[:, cut]

    def fill(peer, _):
        for c in range(cap):
            block = list_ref[c, 0, peer]
            data = full_ref[pl.ds(pl.multiple_of(block * 8, 8), 8), :]
            out_ref[pl.ds(peer * (cap * 6) + c * 6, 6), :] = data[:6]
        return 0

    lax.fori_loop(0, peers, fill, 0, unroll=2)


def interact(count, item, tt, st, ww, acc, dsc, ksc):
    most = tt.shape[0] - 1

    def distances(step, side):
        for u in range(GROUP):
            target, source = item(step * GROUP + u)
            half = slice((u % 2) * TILE, (u % 2 + 1) * TILE)
            dsc[side, u // 2, :, half] = lax.dot_general(
                st[source], tt[jnp.minimum(target, most)], (((1,), (0,)), ((), ())), preferred_element_type=F32
            )

    def kernels(side):
        for u in range(GROUP // 2):
            inverse = lax.rsqrt(dsc[side, u])
            weight = inverse * inverse * inverse
            high = weight.astype(BF16)
            ksc[side, u, :TILE] = high
            ksc[side, u, TILE:] = (weight - high.astype(F32)).astype(BF16)

    def gather(step, side):
        for u in range(0, GROUP, 2):
            t0, s0 = item(step * GROUP + u)
            t1, s1 = item(step * GROUP + u + 1)
            left = jnp.concatenate([ww[s0], ww[s1]], axis=0)
            left = jnp.concatenate([left, left], axis=1)
            both = lax.dot_general(left, ksc[side, u // 2], (((1,), (0,)), ((), ())), preferred_element_type=F32)
            r0 = pl.ds(pl.multiple_of(t0 * SUMS, SUMS), SUMS)
            acc[r0, :] = acc[r0, :] + both[:SUMS, :TILE]
            r1 = pl.ds(pl.multiple_of(t1 * SUMS, SUMS), SUMS)
            acc[r1, :] = acc[r1, :] + both[SUMS:, TILE:]

    distances(0, 0)
    kernels(0)
    distances(1, 1)

    def turn(index, _):
        for h in range(STEPS):
            step, side = index * STEPS + h, h % 2
            gather(step, side)
            kernels(1 - side)
            distances(step + 2, side)
        return 0

    lax.fori_loop(0, count, turn, 0)


def near_kernel(
    rows, halves, near, kmax, pos_ref, full_ref, near_ref, slot_ref, count_ref,
    acc_ref, tt_ref, item_ref, total_ref, st, ww, stage, dsc, ksc,
):
    tiles = rows * halves
    for r, field in enumerate(target_rows([pos_ref[comp] for comp in range(3)])):
        for half in range(halves):
            stage[pl.ds(half * DEPTH + r, rows, halves * DEPTH), :] = field[:, half * TILE : (half + 1) * TILE]

    def pack(b, _):
        tt_ref[b] = stage[pl.ds(pl.multiple_of(b * DEPTH, DEPTH), DEPTH), :].astype(BF16)
        return 0

    lax.fori_loop(0, tiles, pack, 0, unroll=8)

    def listed(b, at):
        for k in range(kmax):
            item_ref[at + k] = b * 256 + slot_ref[k, b]
        return at + count_ref[b]

    total = lax.fori_loop(0, tiles, listed, 0)
    for k in range((STEPS + 2) * GROUP):
        item_ref[total + k] = tiles * 256
    total_ref[0] = total

    fixed_rows(tiles, stage)
    for half in range(halves):
        parts = [full_ref[pl.ds(half * 8 + comp, rows, halves * 8), :] for comp in range(6)]
        for r, field in source_lines(*source_rows(parts[:3], parts[3:])):
            stage[pl.ds(half * DEPTH + r, rows, halves * DEPTH), :] = field
    pack_sources(tiles, stage, st, ww)
    last = tiles * near - 1

    def item(i):
        i = jnp.minimum(i, last)
        b = lax.div(i, near)
        return b, near_ref[i - b * near, b]

    acc_ref[...] = jnp.zeros_like(acc_ref)
    interact(tiles * near // (STEPS * GROUP), item, tt_ref, st, ww, acc_ref, dsc, ksc)


def far_kernel(
    rows, halves, peers, cap, width_rows,
    pos_ref, recv_ref, tt_ref, near_acc, item_ref, total_ref,
    vel_ref, moved_ref,
    st, ww, stage, acc, dsc, ksc,
):
    fixed_rows(peers * cap, stage)

    def lay(group, _):
        for c in range(cap):
            parts = [
                recv_ref[pl.ds(group * (8 * width_rows) + c * 6 + comp, 8, width_rows), :] for comp in range(6)
            ]
            for r, field in source_lines(*source_rows(parts[:3], parts[3:])):
                stage[pl.ds(group * (8 * cap * DEPTH) + c * DEPTH + r, 8, cap * DEPTH), :] = field
        return 0

    lax.fori_loop(0, peers // 8, lay, 0)
    pack_sources(peers * cap, stage, st, ww)

    def item(i):
        code = item_ref[i]
        return lax.shift_right_logical(code, 8), lax.bitwise_and(code, 255)

    acc[: rows * halves * SUMS, :] = near_acc[...]
    turns = lax.div(total_ref[0] + STEPS * GROUP - 1, STEPS * GROUP)
    interact(turns, item, tt_ref, st, ww, acc, dsc, ksc)

    for half in range(halves):
        cut = slice(half * TILE, (half + 1) * TILE)

        def summed(*lines):
            value = None
            for line in lines:
                term = acc[pl.ds(half * SUMS + line, rows, halves * SUMS), :]
                value = term if value is None else value + term
            return value

        sums = [summed(3 + comp, comp) for comp in range(3)]
        cross = [summed(12 + comp, 9 + comp, 6 + comp) for comp in range(3)]
        point = [pos_ref[comp, :, cut] for comp in range(3)]
        for comp in range(3):
            j, k = (comp + 1) % 3, (comp + 2) % 3
            velocity = sums[j] * point[k] - sums[k] * point[j] - cross[comp]
            vel_ref[comp, :, cut] = velocity
            inflow = inflow_speed if comp == 0 else 0.0
            moved_ref[comp, :, cut] = point[comp] + time_step * (velocity + inflow)


def body(positions, circulation, send_lists, reader_slots, source_counts, near_blocks):
    _, rows, width = positions.shape
    halves = width // TILE
    tiles = rows * halves
    peers = lax.axis_size("turb")
    cap = send_lists.shape[-1]
    kmax = reader_slots.shape[-1]
    near = near_blocks.shape[-1]
    vmem = pl.BlockSpec(memory_space=pltpu.VMEM)
    smem = pl.BlockSpec(memory_space=pltpu.SMEM)
    ages = lax.axis_size("age")
    next_row = lax.ppermute(positions[:, :, :SPAN], "age", [(s, s - 1) for s in range(1, ages)])
    last = (lax.axis_index("age") == ages - 1).astype(jnp.int32).reshape(1)
    width_rows = cap * 6
    params = pltpu.CompilerParams(vmem_limit_bytes=48 << 20)

    anywhere = pl.BlockSpec(memory_space=pltpu.HBM)
    outgoing, full = pl.pallas_call(
        functools.partial(send_kernel, rows, halves, peers, cap),
        out_shape=(
            jax.ShapeDtypeStruct((peers * width_rows, TILE), F32),
            jax.ShapeDtypeStruct((tiles * 8, TILE), F32),
        ),
        in_specs=[anywhere, anywhere, vmem, smem, smem],
        out_specs=(vmem, vmem),
        scratch_shapes=[
            pltpu.VMEM(positions.shape, F32),
            pltpu.VMEM(circulation.shape, F32),
            pltpu.SemaphoreType.DMA((2,)),
        ],
        compiler_params=params,
    )(positions, circulation, next_row, last, send_lists[0, 0].T[:, None])
    incoming = lax.all_to_all(outgoing.reshape(peers, 1, width_rows * TILE), "turb", 0, 0, tiled=True)
    incoming = incoming.reshape(peers * width_rows, TILE)

    pairs = [
        pltpu.VMEM((2, GROUP // 2, TILE, 2 * TILE), F32),
        pltpu.VMEM((2, GROUP // 2, 2 * TILE, 2 * TILE), BF16),
    ]
    near_acc, targets, items, total = pl.pallas_call(
        functools.partial(near_kernel, rows, halves, near, kmax),
        out_shape=(
            jax.ShapeDtypeStruct((tiles * SUMS, TILE), F32),
            jax.ShapeDtypeStruct((tiles, DEPTH, TILE), BF16),
            jax.ShapeDtypeStruct((tiles * kmax + 64,), jnp.int32),
            jax.ShapeDtypeStruct((1,), jnp.int32),
        ),
        in_specs=[vmem, vmem, smem, smem, smem],
        out_specs=(vmem, vmem, smem, smem),
        scratch_shapes=[
            pltpu.VMEM((tiles, TILE, DEPTH), BF16),
            pltpu.VMEM((tiles, SUMS, TILE), BF16),
            pltpu.VMEM((tiles * DEPTH, TILE), F32),
            *pairs,
        ],
        compiler_params=params,
        cost_estimate=pl.CostEstimate(flops=2 * 10**9, bytes_accessed=4 << 20, transcendentals=tiles * near * TILE * TILE),
    )(positions, full, near_blocks[0, 0].T, reader_slots[0, 0].T, source_counts[0, 0])
    return pl.pallas_call(
        functools.partial(far_kernel, rows, halves, peers, cap, width_rows),
        out_shape=(
            jax.ShapeDtypeStruct(positions.shape, F32),
            jax.ShapeDtypeStruct(positions.shape, F32),
        ),
        in_specs=[vmem, vmem, vmem, vmem, smem, smem],
        out_specs=(vmem, vmem),
        scratch_shapes=[
            pltpu.VMEM((peers * cap, TILE, DEPTH), BF16),
            pltpu.VMEM((peers * cap, SUMS, TILE), BF16),
            pltpu.VMEM((peers * cap * DEPTH, TILE), F32),
            pltpu.VMEM(((tiles + 1) * SUMS, TILE), F32),
            *pairs,
        ],
        compiler_params=params,
    )(positions, incoming, targets, near_acc, items, total)


def solution(mesh):
    in_specs = (
        P(None, "turb", "age"),
        P("turb", "age"),
        P("turb", "age", None, None),
        P("turb", "age", None, None),
        P("turb", "age", None),
        P("turb", "age", None, None),
    )
    out_specs = (P(None, "turb", "age"), P(None, "turb", "age"))
    return jax.shard_map(body, mesh=mesh, in_specs=in_specs, out_specs=out_specs, check_vma=False)
```

```python
import functools

import jax
import jax.numpy as jnp
from jax import lax
from jax.experimental import pallas as pl
from jax.experimental.pallas import tpu as pltpu
from jax.sharding import PartitionSpec as P

SPAN = 64
TILE = 128
time_step = 0.1
core_square = 0.25
inflow_speed = 1.0
inv_four_pi = 0.07957747154594767
GROUP = 8
STEPS = 4
DEPTH = 32
SUMS = 16
F32 = jnp.float32
BF16 = jnp.bfloat16


def split3(value):
    first = value.astype(BF16).astype(F32)
    rest = value - first
    second = rest.astype(BF16).astype(F32)
    third = (rest - second).astype(BF16).astype(F32)
    return first, second, third


def source_rows(middle, strength):
    parts = [split3(-2.0 * middle[comp]) for comp in range(3)]
    square = middle[0] * middle[0] + middle[1] * middle[1] + middle[2] * middle[2] + core_square
    squares = split3(square)
    near_rows = [parts[comp][0] for comp in range(3)] + [parts[comp][1] for comp in range(3)]
    near_rows += [squares[0], squares[1]] + [parts[comp][2] for comp in range(3)] + [squares[2]]
    w1, w2, w = [], [], []
    for comp in range(3):
        first, second, _ = split3(inv_four_pi * strength[comp])
        w1.append(first)
        w2.append(second)
        w.append(first + second)
    u = [
        split3(w[1] * middle[2] - w[2] * middle[1]),
        split3(w[2] * middle[0] - w[0] * middle[2]),
        split3(w[0] * middle[1] - w[1] * middle[0]),
    ]
    strength_rows = w1 + w2 + [u[comp][level] for level in range(3) for comp in range(3)]
    return near_rows, strength_rows


def target_rows(point):
    parts = [split3(point[comp]) for comp in range(3)]
    square = point[0] * point[0] + point[1] * point[1] + point[2] * point[2]
    one, zero = jnp.ones_like(square), jnp.zeros_like(square)
    first, second, third = ([parts[comp][level] for comp in range(3)] for level in range(3))
    return (
        first + first + [one, one]
        + second + second + [zero, zero]
        + third + [zero] * 5
        + first + [one] + list(split3(square)) + [zero]
    )


def fixed_rows(blocks, stage):
    line = lax.broadcasted_iota(jnp.int32, (8, TILE), 0)
    ones = jnp.where((line >= 4) & (line < 7), 1.0, 0.0)

    def fill(b, _):
        stage[pl.ds(pl.multiple_of(b * DEPTH + 8, 8), 8), :] = ones
        stage[pl.ds(pl.multiple_of(b * DEPTH + 24, 8), 8), :] = jnp.zeros_like(ones)
        return 0

    lax.fori_loop(0, blocks, fill, 0, unroll=8)


def pack_sources(blocks, stage, st, ww):
    def pack(b, _):
        base = pl.multiple_of(b * DEPTH, DEPTH)
        top = stage[pl.ds(base, 8), :]
        rest = stage[pl.ds(base + 8, 8), :]
        st[b] = jnp.concatenate([top, top, top, rest], axis=0).astype(BF16).T
        ww[b] = stage[pl.ds(base + 16, SUMS), :].astype(BF16)
        return 0

    lax.fori_loop(0, blocks, pack, 0, unroll=32)


def source_lines(near_rows, strength_rows):
    return list(enumerate(near_rows)) + [(16 + r, row) for r, row in enumerate(strength_rows)]


def send_kernel(
    rows, halves, peers, cap, pos_ref, circ_ref, next_ref, last_ref, list_ref, out_ref, full_ref
):
    ends = last_ref[0] == 1
    for comp in range(3):
        here = pos_ref[comp]
        beyond = jnp.where(ends, here[:, -SPAN:], next_ref[comp])
        segment = jnp.concatenate([here[:, SPAN:], beyond], axis=1) - here
        middle = here + 0.5 * segment
        strength = circ_ref[...] * segment
        for half in range(halves):
            cut = slice(half * TILE, (half + 1) * TILE)
            full_ref[pl.ds(half * 8 + comp, rows, halves * 8), :] = middle[:, cut]
            full_ref[pl.ds(half * 8 + 3 + comp, rows, halves * 8), :] = strength[:, cut]

    def fill(peer, _):
        for c in range(cap):
            block = list_ref[0, c, 0, peer]
            data = full_ref[pl.ds(pl.multiple_of(block * 8, 8), 8), :]
            out_ref[pl.ds(peer * (cap * 6) + c * 6, 6), :] = data[:6]
        return 0

    lax.fori_loop(0, peers, fill, 0, unroll=2)


def interact(count, item, tt, st, ww, acc, dsc, ksc):
    most = tt.shape[0] - 1

    def distances(step, side):
        for u in range(GROUP):
            target, source = item(step * GROUP + u)
            half = slice((u % 2) * TILE, (u % 2 + 1) * TILE)
            dsc[side, u // 2, :, half] = lax.dot_general(
                st[source], tt[jnp.minimum(target, most)], (((1,), (0,)), ((), ())), preferred_element_type=F32
            )

    def kernels(side):
        for u in range(GROUP // 2):
            inverse = lax.rsqrt(dsc[side, u])
            weight = inverse * inverse * inverse
            high = weight.astype(BF16)
            ksc[side, u, :TILE] = high
            ksc[side, u, TILE:] = (weight - high.astype(F32)).astype(BF16)

    def gather(step, side):
        for u in range(0, GROUP, 2):
            t0, s0 = item(step * GROUP + u)
            t1, s1 = item(step * GROUP + u + 1)
            left = jnp.concatenate([ww[s0], ww[s1]], axis=0)
            left = jnp.concatenate([left, left], axis=1)
            both = lax.dot_general(left, ksc[side, u // 2], (((1,), (0,)), ((), ())), preferred_element_type=F32)
            r0 = pl.ds(pl.multiple_of(t0 * SUMS, SUMS), SUMS)
            acc[r0, :] = acc[r0, :] + both[:SUMS, :TILE]
            r1 = pl.ds(pl.multiple_of(t1 * SUMS, SUMS), SUMS)
            acc[r1, :] = acc[r1, :] + both[SUMS:, TILE:]

    distances(0, 0)
    kernels(0)
    distances(1, 1)

    def turn(index, _):
        for h in range(STEPS):
            step, side = index * STEPS + h, h % 2
            gather(step, side)
            kernels(1 - side)
            distances(step + 2, side)
        return 0

    lax.fori_loop(0, count, turn, 0)


def near_kernel(
    rows, halves, near, kmax, pos_ref, full_ref, near_ref, slot_ref, count_ref,
    acc_ref, tt_ref, item_ref, total_ref, st, ww, stage, dsc, ksc,
):
    tiles = rows * halves
    for r, field in enumerate(target_rows([pos_ref[comp] for comp in range(3)])):
        for half in range(halves):
            stage[pl.ds(half * DEPTH + r, rows, halves * DEPTH), :] = field[:, half * TILE : (half + 1) * TILE]

    def pack(b, _):
        tt_ref[b] = stage[pl.ds(pl.multiple_of(b * DEPTH, DEPTH), DEPTH), :].astype(BF16)
        return 0

    lax.fori_loop(0, tiles, pack, 0, unroll=8)

    def listed(b, at):
        for k in range(kmax):
            item_ref[at + k] = b * 256 + slot_ref[k, b]
        return at + count_ref[b]

    total = lax.fori_loop(0, tiles, listed, 0)
    for k in range((STEPS + 2) * GROUP):
        item_ref[total + k] = tiles * 256
    total_ref[0] = total

    fixed_rows(tiles, stage)
    for half in range(halves):
        parts = [full_ref[pl.ds(half * 8 + comp, rows, halves * 8), :] for comp in range(6)]
        for r, field in source_lines(*source_rows(parts[:3], parts[3:])):
            stage[pl.ds(half * DEPTH + r, rows, halves * DEPTH), :] = field
    pack_sources(tiles, stage, st, ww)
    last = tiles * near - 1

    def item(i):
        i = jnp.minimum(i, last)
        b = lax.div(i, near)
        return b, near_ref[i - b * near, b]

    acc_ref[...] = jnp.zeros_like(acc_ref)
    interact(tiles * near // (STEPS * GROUP), item, tt_ref, st, ww, acc_ref, dsc, ksc)


def far_kernel(
    rows, halves, peers, cap, width_rows,
    pos_ref, recv_ref, tt_ref, near_acc, item_ref, total_ref,
    vel_ref, moved_ref,
    st, ww, stage, acc, dsc, ksc,
):
    fixed_rows(peers * cap, stage)

    def lay(group, _):
        for c in range(cap):
            parts = [
                recv_ref[pl.ds(group * (8 * width_rows) + c * 6 + comp, 8, width_rows), :] for comp in range(6)
            ]
            for r, field in source_lines(*source_rows(parts[:3], parts[3:])):
                stage[pl.ds(group * (8 * cap * DEPTH) + c * DEPTH + r, 8, cap * DEPTH), :] = field
        return 0

    lax.fori_loop(0, peers // 8, lay, 0)
    pack_sources(peers * cap, stage, st, ww)

    def item(i):
        code = item_ref[i]
        return lax.shift_right_logical(code, 8), lax.bitwise_and(code, 255)

    acc[: rows * halves * SUMS, :] = near_acc[...]
    turns = lax.div(total_ref[0] + STEPS * GROUP - 1, STEPS * GROUP)
    interact(turns, item, tt_ref, st, ww, acc, dsc, ksc)

    for half in range(halves):
        cut = slice(half * TILE, (half + 1) * TILE)

        def summed(*lines):
            value = None
            for line in lines:
                term = acc[pl.ds(half * SUMS + line, rows, halves * SUMS), :]
                value = term if value is None else value + term
            return value

        sums = [summed(3 + comp, comp) for comp in range(3)]
        cross = [summed(12 + comp, 9 + comp, 6 + comp) for comp in range(3)]
        point = [pos_ref[comp, :, cut] for comp in range(3)]
        for comp in range(3):
            j, k = (comp + 1) % 3, (comp + 2) % 3
            velocity = sums[j] * point[k] - sums[k] * point[j] - cross[comp]
            vel_ref[comp, :, cut] = velocity
            inflow = inflow_speed if comp == 0 else 0.0
            moved_ref[comp, :, cut] = point[comp] + time_step * (velocity + inflow)


def body(positions, circulation, send_lists, reader_slots, source_counts, near_blocks):
    _, rows, width = positions.shape
    halves = width // TILE
    tiles = rows * halves
    peers = lax.axis_size("turb")
    cap = send_lists.shape[-1]
    kmax = reader_slots.shape[-1]
    near = near_blocks.shape[-1]
    vmem = pl.BlockSpec(memory_space=pltpu.VMEM)
    smem = pl.BlockSpec(memory_space=pltpu.SMEM)
    ages = lax.axis_size("age")
    next_row = lax.ppermute(positions[:, :, :SPAN], "age", [(s, s - 1) for s in range(1, ages)])
    last = (lax.axis_index("age") == ages - 1).astype(jnp.int32).reshape(1)
    width_rows = cap * 6
    params = pltpu.CompilerParams(vmem_limit_bytes=48 << 20)

    outgoing, full = pl.pallas_call(
        functools.partial(send_kernel, rows, halves, peers, cap),
        out_shape=(
            jax.ShapeDtypeStruct((peers * width_rows, TILE), F32),
            jax.ShapeDtypeStruct((tiles * 8, TILE), F32),
        ),
        in_specs=[vmem, vmem, vmem, smem, smem],
        out_specs=(vmem, vmem),
        compiler_params=params,
    )(positions, circulation, next_row, last, send_lists.transpose(0, 3, 1, 2))
    incoming = lax.all_to_all(outgoing.reshape(peers, 1, width_rows * TILE), "turb", 0, 0, tiled=True)
    incoming = incoming.reshape(peers * width_rows, TILE)

    pairs = [
        pltpu.VMEM((2, GROUP // 2, TILE, 2 * TILE), F32),
        pltpu.VMEM((2, GROUP // 2, 2 * TILE, 2 * TILE), BF16),
    ]
    near_acc, targets, items, total = pl.pallas_call(
        functools.partial(near_kernel, rows, halves, near, kmax),
        out_shape=(
            jax.ShapeDtypeStruct((tiles * SUMS, TILE), F32),
            jax.ShapeDtypeStruct((tiles, DEPTH, TILE), BF16),
            jax.ShapeDtypeStruct((tiles * kmax + 64,), jnp.int32),
            jax.ShapeDtypeStruct((1,), jnp.int32),
        ),
        in_specs=[vmem, vmem, smem, smem, smem],
        out_specs=(vmem, vmem, smem, smem),
        scratch_shapes=[
            pltpu.VMEM((tiles, TILE, DEPTH), BF16),
            pltpu.VMEM((tiles, SUMS, TILE), BF16),
            pltpu.VMEM((tiles * DEPTH, TILE), F32),
            *pairs,
        ],
        compiler_params=params,
        cost_estimate=pl.CostEstimate(flops=2 * 10**9, bytes_accessed=4 << 20, transcendentals=tiles * near * TILE * TILE),
    )(positions, full, near_blocks[0, 0].T, reader_slots[0, 0].T, source_counts[0, 0])
    return pl.pallas_call(
        functools.partial(far_kernel, rows, halves, peers, cap, width_rows),
        out_shape=(
            jax.ShapeDtypeStruct(positions.shape, F32),
            jax.ShapeDtypeStruct(positions.shape, F32),
        ),
        in_specs=[vmem, vmem, vmem, vmem, smem, smem],
        out_specs=(vmem, vmem),
        scratch_shapes=[
            pltpu.VMEM((peers * cap, TILE, DEPTH), BF16),
            pltpu.VMEM((peers * cap, SUMS, TILE), BF16),
            pltpu.VMEM((peers * cap * DEPTH, TILE), F32),
            pltpu.VMEM(((tiles + 1) * SUMS, TILE), F32),
            *pairs,
        ],
        compiler_params=params,
    )(positions, incoming, targets, near_acc, items, total)


def solution(mesh):
    in_specs = (
        P(None, "turb", "age"),
        P("turb", "age"),
        P("turb", "age", None, None),
        P("turb", "age", None, None),
        P("turb", "age", None),
        P("turb", "age", None, None),
    )
    out_specs = (P(None, "turb", "age"), P(None, "turb", "age"))
    return jax.shard_map(body, mesh=mesh, in_specs=in_specs, out_specs=out_specs, check_vma=False)
```

```python
import functools

import jax
import jax.numpy as jnp
from jax import lax
from jax.experimental import pallas as pl
from jax.experimental.pallas import tpu as pltpu
from jax.sharding import PartitionSpec as P

SPAN = 64
TILE = 128
time_step = 0.1
core_square = 0.25
inflow_speed = 1.0
inv_four_pi = 0.07957747154594767
GROUP = 8
STEPS = 6
DEPTH = 32
SUMS = 16
F32 = jnp.float32
BF16 = jnp.bfloat16


def split3(value):
    first = value.astype(BF16).astype(F32)
    rest = value - first
    second = rest.astype(BF16).astype(F32)
    third = (rest - second).astype(BF16).astype(F32)
    return first, second, third


def source_rows(middle, strength):
    parts = [split3(-2.0 * middle[comp]) for comp in range(3)]
    square = middle[0] * middle[0] + middle[1] * middle[1] + middle[2] * middle[2] + core_square
    squares = split3(square)
    near_rows = [parts[comp][0] for comp in range(3)] + [parts[comp][1] for comp in range(3)]
    near_rows += [squares[0], squares[1]] + [parts[comp][2] for comp in range(3)] + [squares[2]]
    w1, w2, w = [], [], []
    for comp in range(3):
        first, second, _ = split3(inv_four_pi * strength[comp])
        w1.append(first)
        w2.append(second)
        w.append(first + second)
    u = [
        split3(w[1] * middle[2] - w[2] * middle[1]),
        split3(w[2] * middle[0] - w[0] * middle[2]),
        split3(w[0] * middle[1] - w[1] * middle[0]),
    ]
    strength_rows = w1 + w2 + [u[comp][level] for level in range(3) for comp in range(3)]
    return near_rows, strength_rows


def target_lines(point):
    parts = [split3(point[comp]) for comp in range(3)]
    square = point[0] * point[0] + point[1] * point[1] + point[2] * point[2]
    lines = [(28 + level, row) for level, row in enumerate(split3(square))]
    for comp in range(3):
        first, second, third = parts[comp]
        lines += [(comp, first), (3 + comp, first), (8 + comp, second), (11 + comp, second)]
        lines += [(16 + comp, third), (24 + comp, first)]
    return lines


def fixed_rows(blocks, stage):
    line = lax.broadcasted_iota(jnp.int32, (8, TILE), 0)
    ones = jnp.where((line >= 4) & (line < 7), 1.0, 0.0)

    def fill(b, _):
        stage[pl.ds(pl.multiple_of(b * DEPTH + 8, 8), 8), :] = ones
        stage[pl.ds(pl.multiple_of(b * DEPTH + 24, 8), 8), :] = jnp.zeros_like(ones)
        return 0

    lax.fori_loop(0, blocks, fill, 0, unroll=8)


def pack_sources(blocks, stage, st, ww):
    def pack(b, _):
        base = pl.multiple_of(b * DEPTH, DEPTH)
        top = stage[pl.ds(base, 8), :]
        rest = stage[pl.ds(base + 8, 8), :]
        st[b] = jnp.concatenate([top, top, top, rest], axis=0).astype(BF16).T
        ww[b] = stage[pl.ds(base + 16, SUMS), :].astype(BF16)
        return 0

    lax.fori_loop(0, blocks, pack, 0, unroll=32)


def source_lines(near_rows, strength_rows):
    return list(enumerate(near_rows)) + [(16 + r, row) for r, row in enumerate(strength_rows)]


def send_kernel(
    rows, halves, peers, cap, pos_ref, circ_ref, next_ref, last_ref, list_ref, out_ref, full_ref
):
    ends = last_ref[0] == 1
    for comp in range(3):
        here = pos_ref[comp]
        beyond = jnp.where(ends, here[:, -SPAN:], next_ref[comp])
        segment = jnp.concatenate([here[:, SPAN:], beyond], axis=1) - here
        middle = here + 0.5 * segment
        strength = circ_ref[...] * segment
        for half in range(halves):
            cut = slice(half * TILE, (half + 1) * TILE)
            full_ref[pl.ds(half * 8 + comp, rows, halves * 8), :] = middle[:, cut]
            full_ref[pl.ds(half * 8 + 3 + comp, rows, halves * 8), :] = strength[:, cut]

    def fill(peer, _):
        for c in range(cap):
            block = list_ref[0, c, 0, peer]
            data = full_ref[pl.ds(pl.multiple_of(block * 8, 8), 8), :]
            out_ref[pl.ds(peer * (cap * 6) + c * 6, 6), :] = data[:6]
        return 0

    lax.fori_loop(0, peers, fill, 0, unroll=2)


def interact(count, item, tt, st, ww, acc, dsc, ksc):
    most = tt.shape[0] - 1

    def distances(step, side):
        for u in range(GROUP):
            target, source = item(step * GROUP + u)
            half = slice((u % 2) * TILE, (u % 2 + 1) * TILE)
            dsc[side, u // 2, :, half] = lax.dot_general(
                st[source], tt[jnp.minimum(target, most)], (((1,), (0,)), ((), ())), preferred_element_type=F32
            )

    def kernels(side):
        for u in range(GROUP // 2):
            inverse = lax.rsqrt(dsc[side, u])
            weight = inverse * inverse * inverse
            high = weight.astype(BF16)
            ksc[side, u, :TILE] = high
            ksc[side, u, TILE:] = (weight - high.astype(F32)).astype(BF16)

    def gather(step, side):
        for u in range(0, GROUP, 2):
            t0, s0 = item(step * GROUP + u)
            t1, s1 = item(step * GROUP + u + 1)
            left = jnp.concatenate([ww[s0], ww[s1]], axis=0)
            left = jnp.concatenate([left, left], axis=1)
            both = lax.dot_general(left, ksc[side, u // 2], (((1,), (0,)), ((), ())), preferred_element_type=F32)
            r0 = pl.ds(pl.multiple_of(t0 * SUMS, SUMS), SUMS)
            acc[r0, :] = acc[r0, :] + both[:SUMS, :TILE]
            r1 = pl.ds(pl.multiple_of(t1 * SUMS, SUMS), SUMS)
            acc[r1, :] = acc[r1, :] + both[SUMS:, TILE:]

    distances(0, 0)
    kernels(0)
    distances(1, 1)

    def turn(index, _):
        for h in range(STEPS):
            step, side = index * STEPS + h, h % 2
            gather(step, side)
            kernels(1 - side)
            distances(step + 2, side)
        return 0

    lax.fori_loop(0, count, turn, 0)


def near_kernel(
    rows, halves, near, kmax, pos_ref, full_ref, near_ref, slot_ref, count_ref,
    acc_ref, tt_ref, item_ref, total_ref, st, ww, stage, dsc, ksc,
):
    tiles = rows * halves
    line = lax.broadcasted_iota(jnp.int32, (DEPTH, TILE), 0)
    ones = jnp.where((line == 6) | (line == 7) | (line == 27), 1.0, 0.0)

    def blank(b, _):
        stage[pl.ds(pl.multiple_of(b * DEPTH, DEPTH), DEPTH), :] = ones
        return 0

    lax.fori_loop(0, tiles, blank, 0, unroll=8)
    for r, field in target_lines([pos_ref[comp] for comp in range(3)]):
        for half in range(halves):
            stage[pl.ds(half * DEPTH + r, rows, halves * DEPTH), :] = field[:, half * TILE : (half + 1) * TILE]

    def pack(b, _):
        tt_ref[b] = stage[pl.ds(pl.multiple_of(b * DEPTH, DEPTH), DEPTH), :].astype(BF16)
        return 0

    lax.fori_loop(0, tiles, pack, 0, unroll=8)

    def listed(b, at):
        for k in range(kmax):
            item_ref[at + k] = b * 256 + slot_ref[k, b]
        return at + count_ref[b]

    total = lax.fori_loop(0, tiles, listed, 0)
    for k in range((STEPS + 2) * GROUP):
        item_ref[total + k] = tiles * 256
    total_ref[0] = total

    fixed_rows(tiles, stage)
    for half in range(halves):
        parts = [full_ref[pl.ds(half * 8 + comp, rows, halves * 8), :] for comp in range(6)]
        for r, field in source_lines(*source_rows(parts[:3], parts[3:])):
            stage[pl.ds(half * DEPTH + r, rows, halves * DEPTH), :] = field
    pack_sources(tiles, stage, st, ww)
    last = tiles * near - 1

    def item(i):
        i = jnp.minimum(i, last)
        b = lax.div(i, near)
        return b, near_ref[i - b * near, b]

    acc_ref[...] = jnp.zeros_like(acc_ref)
    interact(tiles * near // (STEPS * GROUP), item, tt_ref, st, ww, acc_ref, dsc, ksc)


def far_kernel(
    rows, halves, peers, cap, width_rows,
    pos_ref, recv_ref, tt_ref, near_acc, item_ref, total_ref,
    vel_ref, moved_ref,
    st, ww, stage, acc, dsc, ksc,
):
    fixed_rows(peers * cap, stage)

    def lay(group, _):
        for c in range(cap):
            parts = [
                recv_ref[pl.ds(group * (8 * width_rows) + c * 6 + comp, 8, width_rows), :] for comp in range(6)
            ]
            for r, field in source_lines(*source_rows(parts[:3], parts[3:])):
                stage[pl.ds(group * (8 * cap * DEPTH) + c * DEPTH + r, 8, cap * DEPTH), :] = field
        return 0

    lax.fori_loop(0, peers // 8, lay, 0)
    pack_sources(peers * cap, stage, st, ww)

    def item(i):
        code = item_ref[i]
        return lax.shift_right_logical(code, 8), lax.bitwise_and(code, 255)

    acc[: rows * halves * SUMS, :] = near_acc[...]
    turns = lax.div(total_ref[0] + STEPS * GROUP - 1, STEPS * GROUP)
    interact(turns, item, tt_ref, st, ww, acc, dsc, ksc)

    for half in range(halves):
        cut = slice(half * TILE, (half + 1) * TILE)

        def summed(*lines):
            value = None
            for line in lines:
                term = acc[pl.ds(half * SUMS + line, rows, halves * SUMS), :]
                value = term if value is None else value + term
            return value

        sums = [summed(3 + comp, comp) for comp in range(3)]
        cross = [summed(12 + comp, 9 + comp, 6 + comp) for comp in range(3)]
        point = [pos_ref[comp, :, cut] for comp in range(3)]
        for comp in range(3):
            j, k = (comp + 1) % 3, (comp + 2) % 3
            velocity = sums[j] * point[k] - sums[k] * point[j] - cross[comp]
            vel_ref[comp, :, cut] = velocity
            inflow = inflow_speed if comp == 0 else 0.0
            moved_ref[comp, :, cut] = point[comp] + time_step * (velocity + inflow)


def body(positions, circulation, send_lists, reader_slots, source_counts, near_blocks):
    _, rows, width = positions.shape
    halves = width // TILE
    tiles = rows * halves
    peers = lax.axis_size("turb")
    cap = send_lists.shape[-1]
    kmax = reader_slots.shape[-1]
    near = near_blocks.shape[-1]
    vmem = pl.BlockSpec(memory_space=pltpu.VMEM)
    smem = pl.BlockSpec(memory_space=pltpu.SMEM)
    ages = lax.axis_size("age")
    next_row = lax.ppermute(positions[:, :, :SPAN], "age", [(s, s - 1) for s in range(1, ages)])
    last = (lax.axis_index("age") == ages - 1).astype(jnp.int32).reshape(1)
    width_rows = cap * 6
    params = pltpu.CompilerParams(vmem_limit_bytes=48 << 20)

    outgoing, full = pl.pallas_call(
        functools.partial(send_kernel, rows, halves, peers, cap),
        out_shape=(
            jax.ShapeDtypeStruct((peers * width_rows, TILE), F32),
            jax.ShapeDtypeStruct((tiles * 8, TILE), F32),
        ),
        in_specs=[vmem, vmem, vmem, smem, smem],
        out_specs=(vmem, vmem),
        compiler_params=params,
    )(positions, circulation, next_row, last, send_lists.transpose(0, 3, 1, 2))
    incoming = lax.all_to_all(outgoing.reshape(peers, 1, width_rows * TILE), "turb", 0, 0, tiled=True)
    incoming = incoming.reshape(peers * width_rows, TILE)

    pairs = [
        pltpu.VMEM((2, GROUP // 2, TILE, 2 * TILE), F32),
        pltpu.VMEM((2, GROUP // 2, 2 * TILE, 2 * TILE), BF16),
    ]
    near_acc, targets, items, total = pl.pallas_call(
        functools.partial(near_kernel, rows, halves, near, kmax),
        out_shape=(
            jax.ShapeDtypeStruct((tiles * SUMS, TILE), F32),
            jax.ShapeDtypeStruct((tiles, DEPTH, TILE), BF16),
            jax.ShapeDtypeStruct((tiles * kmax + 64,), jnp.int32),
            jax.ShapeDtypeStruct((1,), jnp.int32),
        ),
        in_specs=[vmem, vmem, smem, smem, smem],
        out_specs=(vmem, vmem, smem, smem),
        scratch_shapes=[
            pltpu.VMEM((tiles, TILE, DEPTH), BF16),
            pltpu.VMEM((tiles, SUMS, TILE), BF16),
            pltpu.VMEM((tiles * DEPTH, TILE), F32),
            *pairs,
        ],
        compiler_params=params,
        cost_estimate=pl.CostEstimate(flops=2 * 10**9, bytes_accessed=4 << 20, transcendentals=tiles * near * TILE * TILE),
    )(positions, full, near_blocks[0, 0].T, reader_slots[0, 0].T, source_counts[0, 0])
    return pl.pallas_call(
        functools.partial(far_kernel, rows, halves, peers, cap, width_rows),
        out_shape=(
            jax.ShapeDtypeStruct(positions.shape, F32),
            jax.ShapeDtypeStruct(positions.shape, F32),
        ),
        in_specs=[vmem, vmem, vmem, vmem, smem, smem],
        out_specs=(vmem, vmem),
        scratch_shapes=[
            pltpu.VMEM((peers * cap, TILE, DEPTH), BF16),
            pltpu.VMEM((peers * cap, SUMS, TILE), BF16),
            pltpu.VMEM((peers * cap * DEPTH, TILE), F32),
            pltpu.VMEM(((tiles + 1) * SUMS, TILE), F32),
            *pairs,
        ],
        compiler_params=params,
    )(positions, incoming, targets, near_acc, items, total)


def solution(mesh):
    in_specs = (
        P(None, "turb", "age"),
        P("turb", "age"),
        P("turb", "age", None, None),
        P("turb", "age", None, None),
        P("turb", "age", None),
        P("turb", "age", None, None),
    )
    out_specs = (P(None, "turb", "age"), P(None, "turb", "age"))
    return jax.shard_map(body, mesh=mesh, in_specs=in_specs, out_specs=out_specs, check_vma=False)
```

```python
import functools

import jax
import jax.numpy as jnp
from jax import lax
from jax.experimental import pallas as pl
from jax.experimental.pallas import tpu as pltpu
from jax.sharding import PartitionSpec as P

SPAN = 64
TILE = 128
time_step = 0.1
core_square = 0.25
inflow_speed = 1.0
inv_four_pi = 0.07957747154594767
GROUP = 8
STEPS = 6
DEPTH = 32
SUMS = 16
F32 = jnp.float32
BF16 = jnp.bfloat16


def split3(value):
    first = value.astype(BF16).astype(F32)
    rest = value - first
    second = rest.astype(BF16).astype(F32)
    third = (rest - second).astype(BF16).astype(F32)
    return first, second, third


def source_rows(middle, strength):
    parts = [split3(-2.0 * middle[comp]) for comp in range(3)]
    square = middle[0] * middle[0] + middle[1] * middle[1] + middle[2] * middle[2] + core_square
    squares = split3(square)
    near_rows = [parts[comp][0] for comp in range(3)] + [parts[comp][1] for comp in range(3)]
    near_rows += [squares[0], squares[1]] + [parts[comp][2] for comp in range(3)] + [squares[2]]
    w1, w2, w = [], [], []
    for comp in range(3):
        first, second, _ = split3(inv_four_pi * strength[comp])
        w1.append(first)
        w2.append(second)
        w.append(first + second)
    u = [
        split3(w[1] * middle[2] - w[2] * middle[1]),
        split3(w[2] * middle[0] - w[0] * middle[2]),
        split3(w[0] * middle[1] - w[1] * middle[0]),
    ]
    strength_rows = w1 + w2 + [u[comp][level] for level in range(3) for comp in range(3)]
    return near_rows, strength_rows


def target_lines(point):
    parts = [split3(point[comp]) for comp in range(3)]
    square = point[0] * point[0] + point[1] * point[1] + point[2] * point[2]
    lines = [(28 + level, row) for level, row in enumerate(split3(square))]
    for comp in range(3):
        first, second, third = parts[comp]
        lines += [(comp, first), (3 + comp, first), (8 + comp, second), (11 + comp, second)]
        lines += [(16 + comp, third), (24 + comp, first)]
    return lines


def fixed_rows(blocks, stage):
    line = lax.broadcasted_iota(jnp.int32, (8, TILE), 0)
    ones = jnp.where((line >= 4) & (line < 7), 1.0, 0.0)

    def fill(b, _):
        stage[pl.ds(pl.multiple_of(b * DEPTH + 8, 8), 8), :] = ones
        stage[pl.ds(pl.multiple_of(b * DEPTH + 24, 8), 8), :] = jnp.zeros_like(ones)
        return 0

    lax.fori_loop(0, blocks, fill, 0, unroll=8)


def pack_sources(blocks, stage, st, ww):
    def pack(b, _):
        base = pl.multiple_of(b * DEPTH, DEPTH)
        top = stage[pl.ds(base, 8), :]
        rest = stage[pl.ds(base + 8, 8), :]
        st[b] = jnp.concatenate([top, top, top, rest], axis=0).astype(BF16).T
        ww[b] = stage[pl.ds(base + 16, SUMS), :].astype(BF16)
        return 0

    lax.fori_loop(0, blocks, pack, 0, unroll=32)


def source_lines(near_rows, strength_rows):
    return list(enumerate(near_rows)) + [(16 + r, row) for r, row in enumerate(strength_rows)]


def left_half(rows):
    return lax.broadcasted_iota(jnp.int32, (rows, TILE), 1) < SPAN


def lattice(here, beyond, circ):
    first = left_half(circ.shape[0])
    middles, strengths = [], []
    for comp in range(3):
        following = jnp.where(first, pltpu.roll(here[comp], SPAN, 1), beyond[comp])
        segment = following - here[comp]
        middles.append(here[comp] + 0.5 * segment)
        strengths.append(circ * segment)
    return middles, strengths


def send_kernel(rows, halves, peers, cap, pos_ref, circ_ref, next_ref, last_ref, list_ref, out_ref, full_ref):
    ends = last_ref[0] == 1
    width = halves * TILE
    for half in range(halves):
        cut = slice(half * TILE, (half + 1) * TILE)
        full_ref[pl.ds(half * 8 + 3, rows, halves * 8), :] = circ_ref[:, cut]
        for comp in range(3):
            full_ref[pl.ds(half * 8 + comp, rows, halves * 8), :] = pos_ref[comp, :, cut]
            if half == halves - 1:
                after = jnp.where(ends, pos_ref[comp, :, width - SPAN :], next_ref[comp])
            else:
                after = pos_ref[comp, :, (half + 1) * TILE : (half + 1) * TILE + SPAN]
            full_ref[pl.ds(half * 8 + 4 + comp, rows, halves * 8), :] = jnp.concatenate([after, after], axis=1)
    first = left_half(3)

    def fill(peer, _):
        base = peer * (cap * 11 // 2)
        after = None
        for c in range(cap):
            block = list_ref[0, c, 0, peer]
            data = full_ref[pl.ds(pl.multiple_of(block * 8, 8), 8), :]
            out_ref[pl.ds(base + c * 4, 4), :] = data[:4]
            if c % 2 == 0:
                after = data[4:7]
            else:
                out_ref[pl.ds(base + cap * 4 + c // 2 * 3, 3), :] = jnp.where(first, after, data[4:7])
        return 0

    lax.fori_loop(0, peers, fill, 0, unroll=2)


def interact(count, item, tt, st, ww, acc, dsc, ksc):
    most = tt.shape[0] - 1

    def distances(step, side):
        for u in range(GROUP):
            target, source = item(step * GROUP + u)
            half = slice((u % 2) * TILE, (u % 2 + 1) * TILE)
            dsc[side, u // 2, :, half] = lax.dot_general(
                st[source], tt[jnp.minimum(target, most)], (((1,), (0,)), ((), ())), preferred_element_type=F32
            )

    def kernels(side):
        for u in range(GROUP // 2):
            inverse = lax.rsqrt(dsc[side, u])
            weight = inverse * inverse * inverse
            high = weight.astype(BF16)
            ksc[side, u, :TILE] = high
            ksc[side, u, TILE:] = (weight - high.astype(F32)).astype(BF16)

    def gather(step, side):
        for u in range(0, GROUP, 2):
            t0, s0 = item(step * GROUP + u)
            t1, s1 = item(step * GROUP + u + 1)
            left = jnp.concatenate([ww[s0], ww[s1]], axis=0)
            left = jnp.concatenate([left, left], axis=1)
            both = lax.dot_general(left, ksc[side, u // 2], (((1,), (0,)), ((), ())), preferred_element_type=F32)
            r0 = pl.ds(pl.multiple_of(t0 * SUMS, SUMS), SUMS)
            acc[r0, :] = acc[r0, :] + both[:SUMS, :TILE]
            r1 = pl.ds(pl.multiple_of(t1 * SUMS, SUMS), SUMS)
            acc[r1, :] = acc[r1, :] + both[SUMS:, TILE:]

    distances(0, 0)
    kernels(0)
    distances(1, 1)

    def turn(index, _):
        for h in range(STEPS):
            step, side = index * STEPS + h, h % 2
            gather(step, side)
            kernels(1 - side)
            distances(step + 2, side)
        return 0

    lax.fori_loop(0, count, turn, 0)


def near_kernel(
    rows, halves, near, kmax, pos_ref, full_ref, near_ref, slot_ref, count_ref,
    acc_ref, tt_ref, item_ref, total_ref, st, ww, stage, dsc, ksc,
):
    tiles = rows * halves
    line = lax.broadcasted_iota(jnp.int32, (DEPTH, TILE), 0)
    ones = jnp.where((line == 6) | (line == 7) | (line == 27), 1.0, 0.0)

    def blank(b, _):
        stage[pl.ds(pl.multiple_of(b * DEPTH, DEPTH), DEPTH), :] = ones
        return 0

    lax.fori_loop(0, tiles, blank, 0, unroll=8)
    for r, field in target_lines([pos_ref[comp] for comp in range(3)]):
        for half in range(halves):
            stage[pl.ds(half * DEPTH + r, rows, halves * DEPTH), :] = field[:, half * TILE : (half + 1) * TILE]

    def pack(b, _):
        tt_ref[b] = stage[pl.ds(pl.multiple_of(b * DEPTH, DEPTH), DEPTH), :].astype(BF16)
        return 0

    lax.fori_loop(0, tiles, pack, 0, unroll=8)

    def listed(b, at):
        for k in range(kmax):
            item_ref[at + k] = b * 256 + slot_ref[k, b]
        return at + count_ref[b]

    total = lax.fori_loop(0, tiles, listed, 0)
    for k in range((STEPS + 2) * GROUP):
        item_ref[total + k] = tiles * 256
    total_ref[0] = total

    fixed_rows(tiles, stage)
    for half in range(halves):
        parts = [full_ref[pl.ds(half * 8 + line, rows, halves * 8), :] for line in range(7)]
        for r, field in source_lines(*source_rows(*lattice(parts[:3], parts[4:], parts[3]))):
            stage[pl.ds(half * DEPTH + r, rows, halves * DEPTH), :] = field
    pack_sources(tiles, stage, st, ww)
    last = tiles * near - 1

    def item(i):
        i = jnp.minimum(i, last)
        b = lax.div(i, near)
        return b, near_ref[i - b * near, b]

    acc_ref[...] = jnp.zeros_like(acc_ref)
    interact(tiles * near // (STEPS * GROUP), item, tt_ref, st, ww, acc_ref, dsc, ksc)


def far_kernel(
    rows, halves, peers, cap, width_rows,
    pos_ref, recv_ref, tt_ref, near_acc, item_ref, total_ref,
    vel_ref, moved_ref,
    st, ww, stage, acc, dsc, ksc,
):
    fixed_rows(peers * cap, stage)

    def lay(group, _):
        for c in range(cap):
            base = group * (8 * width_rows)
            lines = [c * 4 + line for line in range(4)] + [cap * 4 + c // 2 * 3 + comp for comp in range(3)]
            parts = [recv_ref[pl.ds(base + line, 8, width_rows), :] for line in lines]
            beyond = parts[4:] if c % 2 else [pltpu.roll(part, SPAN, 1) for part in parts[4:]]
            for r, field in source_lines(*source_rows(*lattice(parts[:3], beyond, parts[3]))):
                stage[pl.ds(group * (8 * cap * DEPTH) + c * DEPTH + r, 8, cap * DEPTH), :] = field
        return 0

    lax.fori_loop(0, peers // 8, lay, 0)
    pack_sources(peers * cap, stage, st, ww)

    def item(i):
        code = item_ref[i]
        return lax.shift_right_logical(code, 8), lax.bitwise_and(code, 255)

    acc[: rows * halves * SUMS, :] = near_acc[...]
    turns = lax.div(total_ref[0] + STEPS * GROUP - 1, STEPS * GROUP)
    interact(turns, item, tt_ref, st, ww, acc, dsc, ksc)

    for half in range(halves):
        cut = slice(half * TILE, (half + 1) * TILE)

        def summed(*lines):
            value = None
            for line in lines:
                term = acc[pl.ds(half * SUMS + line, rows, halves * SUMS), :]
                value = term if value is None else value + term
            return value

        sums = [summed(3 + comp, comp) for comp in range(3)]
        cross = [summed(12 + comp, 9 + comp, 6 + comp) for comp in range(3)]
        point = [pos_ref[comp, :, cut] for comp in range(3)]
        for comp in range(3):
            j, k = (comp + 1) % 3, (comp + 2) % 3
            velocity = sums[j] * point[k] - sums[k] * point[j] - cross[comp]
            vel_ref[comp, :, cut] = velocity
            inflow = inflow_speed if comp == 0 else 0.0
            moved_ref[comp, :, cut] = point[comp] + time_step * (velocity + inflow)


def body(positions, circulation, send_lists, reader_slots, source_counts, near_blocks):
    _, rows, width = positions.shape
    halves = width // TILE
    tiles = rows * halves
    peers = lax.axis_size("turb")
    cap = send_lists.shape[-1]
    kmax = reader_slots.shape[-1]
    near = near_blocks.shape[-1]
    vmem = pl.BlockSpec(memory_space=pltpu.VMEM)
    smem = pl.BlockSpec(memory_space=pltpu.SMEM)
    ages = lax.axis_size("age")
    next_row = lax.ppermute(positions[:, :, :SPAN], "age", [(s, s - 1) for s in range(1, ages)])
    last = (lax.axis_index("age") == ages - 1).astype(jnp.int32).reshape(1)
    width_rows = cap * 11 // 2
    params = pltpu.CompilerParams(vmem_limit_bytes=48 << 20)

    outgoing, full = pl.pallas_call(
        functools.partial(send_kernel, rows, halves, peers, cap),
        out_shape=(
            jax.ShapeDtypeStruct((peers * width_rows, TILE), F32),
            jax.ShapeDtypeStruct((tiles * 8, TILE), F32),
        ),
        in_specs=[vmem, vmem, vmem, smem, smem],
        out_specs=(vmem, vmem),
        compiler_params=params,
    )(positions, circulation, next_row, last, send_lists.transpose(0, 3, 1, 2))
    incoming = lax.all_to_all(outgoing.reshape(peers, 1, width_rows * TILE), "turb", 0, 0, tiled=True)
    incoming = incoming.reshape(peers * width_rows, TILE)

    pairs = [
        pltpu.VMEM((2, GROUP // 2, TILE, 2 * TILE), F32),
        pltpu.VMEM((2, GROUP // 2, 2 * TILE, 2 * TILE), BF16),
    ]
    near_acc, targets, items, total = pl.pallas_call(
        functools.partial(near_kernel, rows, halves, near, kmax),
        out_shape=(
            jax.ShapeDtypeStruct((tiles * SUMS, TILE), F32),
            jax.ShapeDtypeStruct((tiles, DEPTH, TILE), BF16),
            jax.ShapeDtypeStruct((tiles * kmax + 64,), jnp.int32),
            jax.ShapeDtypeStruct((1,), jnp.int32),
        ),
        in_specs=[vmem, vmem, smem, smem, smem],
        out_specs=(vmem, vmem, smem, smem),
        scratch_shapes=[
            pltpu.VMEM((tiles, TILE, DEPTH), BF16),
            pltpu.VMEM((tiles, SUMS, TILE), BF16),
            pltpu.VMEM((tiles * DEPTH, TILE), F32),
            *pairs,
        ],
        compiler_params=params,
        cost_estimate=pl.CostEstimate(flops=2 * 10**9, bytes_accessed=4 << 20, transcendentals=tiles * near * TILE * TILE),
    )(positions, full, near_blocks[0, 0].T, reader_slots[0, 0].T, source_counts[0, 0])
    return pl.pallas_call(
        functools.partial(far_kernel, rows, halves, peers, cap, width_rows),
        out_shape=(
            jax.ShapeDtypeStruct(positions.shape, F32),
            jax.ShapeDtypeStruct(positions.shape, F32),
        ),
        in_specs=[vmem, vmem, vmem, vmem, smem, smem],
        out_specs=(vmem, vmem),
        scratch_shapes=[
            pltpu.VMEM((peers * cap, TILE, DEPTH), BF16),
            pltpu.VMEM((peers * cap, SUMS, TILE), BF16),
            pltpu.VMEM((peers * cap * DEPTH, TILE), F32),
            pltpu.VMEM(((tiles + 1) * SUMS, TILE), F32),
            *pairs,
        ],
        compiler_params=params,
    )(positions, incoming, targets, near_acc, items, total)


def solution(mesh):
    in_specs = (
        P(None, "turb", "age"),
        P("turb", "age"),
        P("turb", "age", None, None),
        P("turb", "age", None, None),
        P("turb", "age", None),
        P("turb", "age", None, None),
    )
    out_specs = (P(None, "turb", "age"), P(None, "turb", "age"))
    return jax.shard_map(body, mesh=mesh, in_specs=in_specs, out_specs=out_specs, check_vma=False)
```

```python
import functools

import jax
import jax.numpy as jnp
from jax import lax
from jax.experimental import pallas as pl
from jax.experimental.pallas import tpu as pltpu
from jax.sharding import PartitionSpec as P

SPAN = 64
TILE = 128
time_step = 0.1
core_square = 0.25
inflow_speed = 1.0
inv_four_pi = 0.07957747154594767
GROUP = 8
STEPS = 6
DEPTH = 32
SUMS = 16
F32 = jnp.float32
BF16 = jnp.bfloat16


def split3(value):
    first = value.astype(BF16).astype(F32)
    rest = value - first
    second = rest.astype(BF16).astype(F32)
    third = (rest - second).astype(BF16).astype(F32)
    return first, second, third


def source_rows(middle, strength):
    parts = [split3(-2.0 * middle[comp]) for comp in range(3)]
    square = middle[0] * middle[0] + middle[1] * middle[1] + middle[2] * middle[2] + core_square
    squares = split3(square)
    near_rows = [parts[comp][0] for comp in range(3)] + [parts[comp][1] for comp in range(3)]
    near_rows += [squares[0], squares[1]] + [parts[comp][2] for comp in range(3)] + [squares[2]]
    w1, w2, w = [], [], []
    for comp in range(3):
        first, second, _ = split3(inv_four_pi * strength[comp])
        w1.append(first)
        w2.append(second)
        w.append(first + second)
    u = [
        split3(w[1] * middle[2] - w[2] * middle[1]),
        split3(w[2] * middle[0] - w[0] * middle[2]),
        split3(w[0] * middle[1] - w[1] * middle[0]),
    ]
    strength_rows = w1 + w2 + [u[comp][level] for level in range(3) for comp in range(3)]
    return near_rows, strength_rows


def target_lines(point):
    parts = [split3(point[comp]) for comp in range(3)]
    square = point[0] * point[0] + point[1] * point[1] + point[2] * point[2]
    lines = [(28 + level, row) for level, row in enumerate(split3(square))]
    for comp in range(3):
        first, second, third = parts[comp]
        lines += [(comp, first), (3 + comp, first), (8 + comp, second), (11 + comp, second)]
        lines += [(16 + comp, third), (24 + comp, first)]
    return lines


def fixed_rows(blocks, stage):
    line = lax.broadcasted_iota(jnp.int32, (8, TILE), 0)
    ones = jnp.where((line >= 4) & (line < 7), 1.0, 0.0)

    def fill(b, _):
        stage[pl.ds(pl.multiple_of(b * DEPTH + 8, 8), 8), :] = ones
        stage[pl.ds(pl.multiple_of(b * DEPTH + 24, 8), 8), :] = jnp.zeros_like(ones)
        return 0

    lax.fori_loop(0, blocks, fill, 0, unroll=8)


def pack_sources(blocks, stage, st, ww):
    def pack(b, _):
        base = pl.multiple_of(b * DEPTH, DEPTH)
        top = stage[pl.ds(base, 8), :]
        rest = stage[pl.ds(base + 8, 8), :]
        st[b] = jnp.concatenate([top, top, top, rest], axis=0).astype(BF16).T
        ww[b] = stage[pl.ds(base + 16, SUMS), :].astype(BF16)
        return 0

    lax.fori_loop(0, blocks, pack, 0, unroll=32)


def source_lines(near_rows, strength_rows):
    return list(enumerate(near_rows)) + [(16 + r, row) for r, row in enumerate(strength_rows)]


def left_half(rows):
    return lax.broadcasted_iota(jnp.int32, (rows, TILE), 1) < SPAN


def lattice(here, beyond, circ):
    first = left_half(circ.shape[0])
    middles, strengths = [], []
    for comp in range(3):
        following = jnp.where(first, pltpu.roll(here[comp], SPAN, 1), beyond[comp])
        segment = following - here[comp]
        middles.append(here[comp] + 0.5 * segment)
        strengths.append(circ * segment)
    return middles, strengths


def send_kernel(rows, halves, peers, cap, pos_ref, circ_ref, next_ref, last_ref, list_ref, out_ref, full_ref):
    ends = last_ref[0] == 1
    width = halves * TILE
    for half in range(halves):
        cut = slice(half * TILE, (half + 1) * TILE)
        full_ref[pl.ds(half * 8 + 3, rows, halves * 8), :] = circ_ref[:, cut]
        for comp in range(3):
            full_ref[pl.ds(half * 8 + comp, rows, halves * 8), :] = pos_ref[comp, :, cut]
            if half == halves - 1:
                after = jnp.where(ends, pos_ref[comp, :, width - SPAN :], next_ref[comp])
            else:
                after = pos_ref[comp, :, (half + 1) * TILE : (half + 1) * TILE + SPAN]
            full_ref[pl.ds(half * 8 + 4 + comp, rows, halves * 8), :] = jnp.concatenate([after, after], axis=1)
    first = left_half(3)

    def fill(peer, _):
        base = peer * (cap * 11 // 2)
        after = None
        for c in range(cap):
            block = list_ref[0, c, 0, peer]
            data = full_ref[pl.ds(pl.multiple_of(block * 8, 8), 8), :]
            out_ref[pl.ds(base + c * 4, 4), :] = data[:4]
            if c % 2 == 0:
                after = data[4:7]
            else:
                out_ref[pl.ds(base + cap * 4 + c // 2 * 3, 3), :] = jnp.where(first, after, data[4:7])
        return 0

    lax.fori_loop(0, peers, fill, 0, unroll=2)


def interact(count, item, tt, st, ww, acc, dsc, ksc):
    most = tt.shape[0] - 1

    def distances(step, side):
        for u in range(GROUP):
            target, source = item(step * GROUP + u)
            half = slice((u % 2) * TILE, (u % 2 + 1) * TILE)
            dsc[side, u // 2, :, half] = lax.dot_general(
                st[source], tt[jnp.minimum(target, most)], (((1,), (0,)), ((), ())), preferred_element_type=F32
            )

    def kernels(side):
        for u in range(GROUP // 2):
            inverse = lax.rsqrt(dsc[side, u])
            weight = inverse * inverse * inverse
            high = weight.astype(BF16)
            ksc[side, u, :TILE] = high
            ksc[side, u, TILE:] = (weight - high.astype(F32)).astype(BF16)

    def gather(step, side):
        for u in range(0, GROUP, 2):
            t0, s0 = item(step * GROUP + u)
            t1, s1 = item(step * GROUP + u + 1)
            left = jnp.concatenate([ww[s0], ww[s1]], axis=0)
            left = jnp.concatenate([left, left], axis=1)
            both = lax.dot_general(left, ksc[side, u // 2], (((1,), (0,)), ((), ())), preferred_element_type=F32)
            r0 = pl.ds(pl.multiple_of(t0 * SUMS, SUMS), SUMS)
            acc[r0, :] = acc[r0, :] + both[:SUMS, :TILE]
            r1 = pl.ds(pl.multiple_of(t1 * SUMS, SUMS), SUMS)
            acc[r1, :] = acc[r1, :] + both[SUMS:, TILE:]

    distances(0, 0)
    kernels(0)
    distances(1, 1)

    def turns(first, times, length):
        def turn(index, _):
            for h in range(length):
                step, side = first + index * length + h, h % 2
                gather(step, side)
                kernels(1 - side)
                distances(step + 2, side)
            return 0

        lax.fori_loop(0, times, turn, 0)

    whole = lax.div(count, STEPS // 2)
    turns(0, whole, STEPS)
    turns(whole * STEPS, count - whole * (STEPS // 2), 2)


def near_kernel(
    rows, halves, near, kmax, pos_ref, full_ref, near_ref, slot_ref, count_ref,
    acc_ref, tt_ref, item_ref, total_ref, st, ww, stage, dsc, ksc,
):
    tiles = rows * halves
    line = lax.broadcasted_iota(jnp.int32, (DEPTH, TILE), 0)
    ones = jnp.where((line == 6) | (line == 7) | (line == 27), 1.0, 0.0)

    def blank(b, _):
        stage[pl.ds(pl.multiple_of(b * DEPTH, DEPTH), DEPTH), :] = ones
        return 0

    lax.fori_loop(0, tiles, blank, 0, unroll=8)
    for r, field in target_lines([pos_ref[comp] for comp in range(3)]):
        for half in range(halves):
            stage[pl.ds(half * DEPTH + r, rows, halves * DEPTH), :] = field[:, half * TILE : (half + 1) * TILE]

    def pack(b, _):
        tt_ref[b] = stage[pl.ds(pl.multiple_of(b * DEPTH, DEPTH), DEPTH), :].astype(BF16)
        return 0

    lax.fori_loop(0, tiles, pack, 0, unroll=8)

    def listed(b, at):
        for k in range(kmax):
            item_ref[at + k] = b * 256 + slot_ref[k, b]
        return at + count_ref[b]

    total = lax.fori_loop(0, tiles, listed, 0)
    for k in range((STEPS + 2) * GROUP):
        item_ref[total + k] = tiles * 256
    total_ref[0] = total

    fixed_rows(tiles, stage)
    for half in range(halves):
        parts = [full_ref[pl.ds(half * 8 + line, rows, halves * 8), :] for line in range(7)]
        for r, field in source_lines(*source_rows(*lattice(parts[:3], parts[4:], parts[3]))):
            stage[pl.ds(half * DEPTH + r, rows, halves * DEPTH), :] = field
    pack_sources(tiles, stage, st, ww)
    last = tiles * near - 1

    def item(i):
        i = jnp.minimum(i, last)
        b = lax.div(i, near)
        return b, near_ref[i - b * near, b]

    acc_ref[...] = jnp.zeros_like(acc_ref)
    interact(-(-tiles * near // (2 * GROUP)), item, tt_ref, st, ww, acc_ref, dsc, ksc)


def far_kernel(
    rows, halves, peers, cap, width_rows,
    pos_ref, recv_ref, tt_ref, near_acc, item_ref, total_ref,
    vel_ref, moved_ref,
    st, ww, stage, acc, dsc, ksc,
):
    fixed_rows(peers * cap, stage)

    def lay(group, _):
        for c in range(cap):
            base = group * (8 * width_rows)
            lines = [c * 4 + line for line in range(4)] + [cap * 4 + c // 2 * 3 + comp for comp in range(3)]
            parts = [recv_ref[pl.ds(base + line, 8, width_rows), :] for line in lines]
            beyond = parts[4:] if c % 2 else [pltpu.roll(part, SPAN, 1) for part in parts[4:]]
            for r, field in source_lines(*source_rows(*lattice(parts[:3], beyond, parts[3]))):
                stage[pl.ds(group * (8 * cap * DEPTH) + c * DEPTH + r, 8, cap * DEPTH), :] = field
        return 0

    lax.fori_loop(0, peers // 8, lay, 0)
    pack_sources(peers * cap, stage, st, ww)

    def item(i):
        code = item_ref[i]
        return lax.shift_right_logical(code, 8), lax.bitwise_and(code, 255)

    acc[: rows * halves * SUMS, :] = near_acc[...]
    pairs = lax.div(total_ref[0] + 2 * GROUP - 1, 2 * GROUP)
    interact(pairs, item, tt_ref, st, ww, acc, dsc, ksc)

    for half in range(halves):
        cut = slice(half * TILE, (half + 1) * TILE)

        def summed(*lines):
            value = None
            for line in lines:
                term = acc[pl.ds(half * SUMS + line, rows, halves * SUMS), :]
                value = term if value is None else value + term
            return value

        sums = [summed(3 + comp, comp) for comp in range(3)]
        cross = [summed(12 + comp, 9 + comp, 6 + comp) for comp in range(3)]
        point = [pos_ref[comp, :, cut] for comp in range(3)]
        for comp in range(3):
            j, k = (comp + 1) % 3, (comp + 2) % 3
            velocity = sums[j] * point[k] - sums[k] * point[j] - cross[comp]
            vel_ref[comp, :, cut] = velocity
            inflow = inflow_speed if comp == 0 else 0.0
            moved_ref[comp, :, cut] = point[comp] + time_step * (velocity + inflow)


def body(positions, circulation, send_lists, reader_slots, source_counts, near_blocks):
    _, rows, width = positions.shape
    halves = width // TILE
    tiles = rows * halves
    peers = lax.axis_size("turb")
    cap = send_lists.shape[-1]
    kmax = reader_slots.shape[-1]
    near = near_blocks.shape[-1]
    vmem = pl.BlockSpec(memory_space=pltpu.VMEM)
    smem = pl.BlockSpec(memory_space=pltpu.SMEM)
    ages = lax.axis_size("age")
    next_row = lax.ppermute(positions[:, :, :SPAN], "age", [(s, s - 1) for s in range(1, ages)])
    last = (lax.axis_index("age") == ages - 1).astype(jnp.int32).reshape(1)
    width_rows = cap * 11 // 2
    params = pltpu.CompilerParams(vmem_limit_bytes=48 << 20)

    outgoing, full = pl.pallas_call(
        functools.partial(send_kernel, rows, halves, peers, cap),
        out_shape=(
            jax.ShapeDtypeStruct((peers * width_rows, TILE), F32),
            jax.ShapeDtypeStruct((tiles * 8, TILE), F32),
        ),
        in_specs=[vmem, vmem, vmem, smem, smem],
        out_specs=(vmem, vmem),
        compiler_params=params,
    )(positions, circulation, next_row, last, send_lists.transpose(0, 3, 1, 2))
    incoming = lax.all_to_all(outgoing.reshape(peers, 1, width_rows * TILE), "turb", 0, 0, tiled=True)
    incoming = incoming.reshape(peers * width_rows, TILE)

    pairs = [
        pltpu.VMEM((2, GROUP // 2, TILE, 2 * TILE), F32),
        pltpu.VMEM((2, GROUP // 2, 2 * TILE, 2 * TILE), BF16),
    ]
    near_acc, targets, items, total = pl.pallas_call(
        functools.partial(near_kernel, rows, halves, near, kmax),
        out_shape=(
            jax.ShapeDtypeStruct((tiles * SUMS, TILE), F32),
            jax.ShapeDtypeStruct((tiles, DEPTH, TILE), BF16),
            jax.ShapeDtypeStruct((tiles * kmax + 64,), jnp.int32),
            jax.ShapeDtypeStruct((1,), jnp.int32),
        ),
        in_specs=[vmem, vmem, smem, smem, smem],
        out_specs=(vmem, vmem, smem, smem),
        scratch_shapes=[
            pltpu.VMEM((tiles, TILE, DEPTH), BF16),
            pltpu.VMEM((tiles, SUMS, TILE), BF16),
            pltpu.VMEM((tiles * DEPTH, TILE), F32),
            *pairs,
        ],
        compiler_params=params,
        cost_estimate=pl.CostEstimate(flops=2 * 10**9, bytes_accessed=4 << 20, transcendentals=tiles * near * TILE * TILE),
    )(positions, full, near_blocks[0, 0].T, reader_slots[0, 0].T, source_counts[0, 0])
    return pl.pallas_call(
        functools.partial(far_kernel, rows, halves, peers, cap, width_rows),
        out_shape=(
            jax.ShapeDtypeStruct(positions.shape, F32),
            jax.ShapeDtypeStruct(positions.shape, F32),
        ),
        in_specs=[vmem, vmem, vmem, vmem, smem, smem],
        out_specs=(vmem, vmem),
        scratch_shapes=[
            pltpu.VMEM((peers * cap, TILE, DEPTH), BF16),
            pltpu.VMEM((peers * cap, SUMS, TILE), BF16),
            pltpu.VMEM((peers * cap * DEPTH, TILE), F32),
            pltpu.VMEM(((tiles + 1) * SUMS, TILE), F32),
            *pairs,
        ],
        compiler_params=params,
    )(positions, incoming, targets, near_acc, items, total)


def solution(mesh):
    in_specs = (
        P(None, "turb", "age"),
        P("turb", "age"),
        P("turb", "age", None, None),
        P("turb", "age", None, None),
        P("turb", "age", None),
        P("turb", "age", None, None),
    )
    out_specs = (P(None, "turb", "age"), P(None, "turb", "age"))
    return jax.shard_map(body, mesh=mesh, in_specs=in_specs, out_specs=out_specs, check_vma=False)
```

```python
import functools

import jax
import jax.numpy as jnp
from jax import lax
from jax.experimental import pallas as pl
from jax.experimental.pallas import tpu as pltpu
from jax.sharding import PartitionSpec as P

SPAN = 64
TILE = 128
time_step = 0.1
core_square = 0.25
inflow_speed = 1.0
inv_four_pi = 0.07957747154594767
GROUP = 8
STEPS = 8
DEPTH = 32
SUMS = 16
F32 = jnp.float32
BF16 = jnp.bfloat16


def split3(value):
    first = value.astype(BF16).astype(F32)
    rest = value - first
    second = rest.astype(BF16).astype(F32)
    third = (rest - second).astype(BF16).astype(F32)
    return first, second, third


def source_rows(middle, strength):
    parts = [split3(-2.0 * middle[comp]) for comp in range(3)]
    square = middle[0] * middle[0] + middle[1] * middle[1] + middle[2] * middle[2] + core_square
    squares = split3(square)
    near_rows = [parts[comp][0] for comp in range(3)] + [parts[comp][1] for comp in range(3)]
    near_rows += [squares[0], squares[1]] + [parts[comp][2] for comp in range(3)] + [squares[2]]
    w1, w2, w = [], [], []
    for comp in range(3):
        first, second, _ = split3(inv_four_pi * strength[comp])
        w1.append(first)
        w2.append(second)
        w.append(first + second)
    u = [
        split3(w[1] * middle[2] - w[2] * middle[1]),
        split3(w[2] * middle[0] - w[0] * middle[2]),
        split3(w[0] * middle[1] - w[1] * middle[0]),
    ]
    strength_rows = w1 + w2 + [u[comp][level] for level in range(3) for comp in range(3)]
    return near_rows, strength_rows


def target_lines(point):
    parts = [split3(point[comp]) for comp in range(3)]
    square = point[0] * point[0] + point[1] * point[1] + point[2] * point[2]
    lines = [(28 + level, row) for level, row in enumerate(split3(square))]
    for comp in range(3):
        first, second, third = parts[comp]
        lines += [(comp, first), (3 + comp, first), (8 + comp, second), (11 + comp, second)]
        lines += [(16 + comp, third), (24 + comp, first)]
    return lines


def fixed_rows(blocks, stage):
    line = lax.broadcasted_iota(jnp.int32, (8, TILE), 0)
    ones = jnp.where((line >= 4) & (line < 7), 1.0, 0.0)

    def fill(b, _):
        stage[pl.ds(pl.multiple_of(b * DEPTH + 8, 8), 8), :] = ones
        stage[pl.ds(pl.multiple_of(b * DEPTH + 24, 8), 8), :] = jnp.zeros_like(ones)
        return 0

    lax.fori_loop(0, blocks, fill, 0, unroll=8)


def pack_sources(blocks, stage, st, ww):
    def pack(b, _):
        base = pl.multiple_of(b * DEPTH, DEPTH)
        top = stage[pl.ds(base, 8), :]
        rest = stage[pl.ds(base + 8, 8), :]
        st[b] = jnp.concatenate([top, top, top, rest], axis=0).astype(BF16).T
        ww[b] = stage[pl.ds(base + 16, SUMS), :].astype(BF16)
        return 0

    lax.fori_loop(0, blocks, pack, 0, unroll=32)


def source_lines(near_rows, strength_rows):
    return list(enumerate(near_rows)) + [(16 + r, row) for r, row in enumerate(strength_rows)]


def left_half(rows):
    return lax.broadcasted_iota(jnp.int32, (rows, TILE), 1) < SPAN


def lattice(here, beyond, circ):
    first = left_half(circ.shape[0])
    middles, strengths = [], []
    for comp in range(3):
        following = jnp.where(first, pltpu.roll(here[comp], SPAN, 1), beyond[comp])
        segment = following - here[comp]
        middles.append(here[comp] + 0.5 * segment)
        strengths.append(circ * segment)
    return middles, strengths


def send_kernel(rows, halves, peers, cap, pos_ref, circ_ref, next_ref, last_ref, list_ref, out_ref, full_ref):
    ends = last_ref[0] == 1
    width = halves * TILE
    for half in range(halves):
        cut = slice(half * TILE, (half + 1) * TILE)
        full_ref[pl.ds(half * 8 + 3, rows, halves * 8), :] = circ_ref[:, cut]
        for comp in range(3):
            full_ref[pl.ds(half * 8 + comp, rows, halves * 8), :] = pos_ref[comp, :, cut]
            if half == halves - 1:
                after = jnp.where(ends, pos_ref[comp, :, width - SPAN :], next_ref[comp])
            else:
                after = pos_ref[comp, :, (half + 1) * TILE : (half + 1) * TILE + SPAN]
            full_ref[pl.ds(half * 8 + 4 + comp, rows, halves * 8), :] = jnp.concatenate([after, after], axis=1)
    first = left_half(3)

    def fill(peer, _):
        base = peer * (cap * 11 // 2)
        after = None
        for c in range(cap):
            block = list_ref[0, c, 0, peer]
            data = full_ref[pl.ds(pl.multiple_of(block * 8, 8), 8), :]
            out_ref[pl.ds(base + c * 4, 4), :] = data[:4]
            if c % 2 == 0:
                after = data[4:7]
            else:
                out_ref[pl.ds(base + cap * 4 + c // 2 * 3, 3), :] = jnp.where(first, after, data[4:7])
        return 0

    lax.fori_loop(0, peers, fill, 0, unroll=2)


def interact(count, item, tt, st, ww, acc, dsc, ksc):
    most = tt.shape[0] - 1

    def distances(step, side):
        for u in range(GROUP):
            target, source = item(step * GROUP + u)
            half = slice((u % 2) * TILE, (u % 2 + 1) * TILE)
            dsc[side, u // 2, :, half] = lax.dot_general(
                st[source], tt[jnp.minimum(target, most)], (((1,), (0,)), ((), ())), preferred_element_type=F32
            )

    def kernels(side):
        for u in range(GROUP // 2):
            inverse = lax.rsqrt(dsc[side, u])
            weight = inverse * inverse * inverse
            high = weight.astype(BF16)
            ksc[side, u, :TILE] = high
            ksc[side, u, TILE:] = (weight - high.astype(F32)).astype(BF16)

    def gather(step, side):
        for u in range(0, GROUP, 2):
            t0, s0 = item(step * GROUP + u)
            t1, s1 = item(step * GROUP + u + 1)
            left = jnp.concatenate([ww[s0], ww[s1]], axis=0)
            left = jnp.concatenate([left, left], axis=1)
            both = lax.dot_general(left, ksc[side, u // 2], (((1,), (0,)), ((), ())), preferred_element_type=F32)
            r0 = pl.ds(pl.multiple_of(t0 * SUMS, SUMS), SUMS)
            acc[r0, :] = acc[r0, :] + both[:SUMS, :TILE]
            r1 = pl.ds(pl.multiple_of(t1 * SUMS, SUMS), SUMS)
            acc[r1, :] = acc[r1, :] + both[SUMS:, TILE:]

    distances(0, 0)
    kernels(0)
    distances(1, 1)

    def turns(first, times, length):
        def turn(index, _):
            for h in range(length):
                step, side = first + index * length + h, h % 2
                gather(step, side)
                kernels(1 - side)
                distances(step + 2, side)
            return 0

        lax.fori_loop(0, times, turn, 0)

    whole = lax.div(count, STEPS // 2)
    turns(0, whole, STEPS)
    turns(whole * STEPS, count - whole * (STEPS // 2), 2)


def near_kernel(
    rows, halves, near, kmax, pos_ref, full_ref, near_ref, slot_ref, count_ref,
    acc_ref, tt_ref, item_ref, total_ref, st, ww, stage, dsc, ksc,
):
    tiles = rows * halves
    line = lax.broadcasted_iota(jnp.int32, (DEPTH, TILE), 0)
    ones = jnp.where((line == 6) | (line == 7) | (line == 27), 1.0, 0.0)

    def blank(b, _):
        stage[pl.ds(pl.multiple_of(b * DEPTH, DEPTH), DEPTH), :] = ones
        return 0

    lax.fori_loop(0, tiles, blank, 0, unroll=8)
    for r, field in target_lines([pos_ref[comp] for comp in range(3)]):
        for half in range(halves):
            stage[pl.ds(half * DEPTH + r, rows, halves * DEPTH), :] = field[:, half * TILE : (half + 1) * TILE]

    def pack(b, _):
        tt_ref[b] = stage[pl.ds(pl.multiple_of(b * DEPTH, DEPTH), DEPTH), :].astype(BF16)
        return 0

    lax.fori_loop(0, tiles, pack, 0, unroll=8)

    def listed(b, at):
        for k in range(kmax):
            item_ref[at + k] = b * 256 + slot_ref[k, b]
        return at + count_ref[b]

    total = lax.fori_loop(0, tiles, listed, 0)
    for k in range(4 * GROUP):
        item_ref[total + k] = tiles * 256
    total_ref[0] = total

    fixed_rows(tiles, stage)
    for half in range(halves):
        parts = [full_ref[pl.ds(half * 8 + line, rows, halves * 8), :] for line in range(7)]
        for r, field in source_lines(*source_rows(*lattice(parts[:3], parts[4:], parts[3]))):
            stage[pl.ds(half * DEPTH + r, rows, halves * DEPTH), :] = field
    pack_sources(tiles, stage, st, ww)
    last = tiles * near - 1

    def item(i):
        i = jnp.minimum(i, last)
        b = lax.div(i, near)
        return b, near_ref[i - b * near, b]

    acc_ref[...] = jnp.zeros_like(acc_ref)
    interact(-(-tiles * near // (2 * GROUP)), item, tt_ref, st, ww, acc_ref, dsc, ksc)


def far_kernel(
    rows, halves, peers, cap, width_rows,
    pos_ref, recv_ref, tt_ref, near_acc, item_ref, total_ref,
    vel_ref, moved_ref,
    st, ww, stage, acc, dsc, ksc,
):
    fixed_rows(peers * cap, stage)

    def lay(group, _):
        for c in range(cap):
            base = group * (8 * width_rows)
            lines = [c * 4 + line for line in range(4)] + [cap * 4 + c // 2 * 3 + comp for comp in range(3)]
            parts = [recv_ref[pl.ds(base + line, 8, width_rows), :] for line in lines]
            beyond = parts[4:] if c % 2 else [pltpu.roll(part, SPAN, 1) for part in parts[4:]]
            for r, field in source_lines(*source_rows(*lattice(parts[:3], beyond, parts[3]))):
                stage[pl.ds(group * (8 * cap * DEPTH) + c * DEPTH + r, 8, cap * DEPTH), :] = field
        return 0

    lax.fori_loop(0, peers // 8, lay, 0)
    pack_sources(peers * cap, stage, st, ww)

    def item(i):
        code = item_ref[i]
        return lax.shift_right_logical(code, 8), lax.bitwise_and(code, 255)

    acc[: rows * halves * SUMS, :] = near_acc[...]
    pairs = lax.div(total_ref[0] + 2 * GROUP - 1, 2 * GROUP)
    interact(pairs, item, tt_ref, st, ww, acc, dsc, ksc)

    for half in range(halves):
        cut = slice(half * TILE, (half + 1) * TILE)

        def summed(*lines):
            value = None
            for line in lines:
                term = acc[pl.ds(half * SUMS + line, rows, halves * SUMS), :]
                value = term if value is None else value + term
            return value

        sums = [summed(3 + comp, comp) for comp in range(3)]
        cross = [summed(12 + comp, 9 + comp, 6 + comp) for comp in range(3)]
        point = [pos_ref[comp, :, cut] for comp in range(3)]
        for comp in range(3):
            j, k = (comp + 1) % 3, (comp + 2) % 3
            velocity = sums[j] * point[k] - sums[k] * point[j] - cross[comp]
            vel_ref[comp, :, cut] = velocity
            inflow = inflow_speed if comp == 0 else 0.0
            moved_ref[comp, :, cut] = point[comp] + time_step * (velocity + inflow)


def body(positions, circulation, send_lists, reader_slots, source_counts, near_blocks):
    _, rows, width = positions.shape
    halves = width // TILE
    tiles = rows * halves
    peers = lax.axis_size("turb")
    cap = send_lists.shape[-1]
    kmax = reader_slots.shape[-1]
    near = near_blocks.shape[-1]
    vmem = pl.BlockSpec(memory_space=pltpu.VMEM)
    smem = pl.BlockSpec(memory_space=pltpu.SMEM)
    ages = lax.axis_size("age")
    next_row = lax.ppermute(positions[:, :, :SPAN], "age", [(s, s - 1) for s in range(1, ages)])
    last = (lax.axis_index("age") == ages - 1).astype(jnp.int32).reshape(1)
    width_rows = cap * 11 // 2
    params = pltpu.CompilerParams(vmem_limit_bytes=48 << 20)

    outgoing, full = pl.pallas_call(
        functools.partial(send_kernel, rows, halves, peers, cap),
        out_shape=(
            jax.ShapeDtypeStruct((peers * width_rows, TILE), F32),
            jax.ShapeDtypeStruct((tiles * 8, TILE), F32),
        ),
        in_specs=[vmem, vmem, vmem, smem, smem],
        out_specs=(vmem, vmem),
        compiler_params=params,
    )(positions, circulation, next_row, last, send_lists.transpose(0, 3, 1, 2))
    incoming = lax.all_to_all(outgoing.reshape(peers, 1, width_rows * TILE), "turb", 0, 0, tiled=True)
    incoming = incoming.reshape(peers * width_rows, TILE)

    pairs = [
        pltpu.VMEM((2, GROUP // 2, TILE, 2 * TILE), F32),
        pltpu.VMEM((2, GROUP // 2, 2 * TILE, 2 * TILE), BF16),
    ]
    near_acc, targets, items, total = pl.pallas_call(
        functools.partial(near_kernel, rows, halves, near, kmax),
        out_shape=(
            jax.ShapeDtypeStruct((tiles * SUMS, TILE), F32),
            jax.ShapeDtypeStruct((tiles, DEPTH, TILE), BF16),
            jax.ShapeDtypeStruct((tiles * kmax + 64,), jnp.int32),
            jax.ShapeDtypeStruct((1,), jnp.int32),
        ),
        in_specs=[vmem, vmem, smem, smem, smem],
        out_specs=(vmem, vmem, smem, smem),
        scratch_shapes=[
            pltpu.VMEM((tiles, TILE, DEPTH), BF16),
            pltpu.VMEM((tiles, SUMS, TILE), BF16),
            pltpu.VMEM((tiles * DEPTH, TILE), F32),
            *pairs,
        ],
        compiler_params=params,
        cost_estimate=pl.CostEstimate(flops=2 * 10**9, bytes_accessed=4 << 20, transcendentals=tiles * near * TILE * TILE),
    )(positions, full, near_blocks[0, 0].T, reader_slots[0, 0].T, source_counts[0, 0])
    return pl.pallas_call(
        functools.partial(far_kernel, rows, halves, peers, cap, width_rows),
        out_shape=(
            jax.ShapeDtypeStruct(positions.shape, F32),
            jax.ShapeDtypeStruct(positions.shape, F32),
        ),
        in_specs=[vmem, vmem, vmem, vmem, smem, smem],
        out_specs=(vmem, vmem),
        scratch_shapes=[
            pltpu.VMEM((peers * cap, TILE, DEPTH), BF16),
            pltpu.VMEM((peers * cap, SUMS, TILE), BF16),
            pltpu.VMEM((peers * cap * DEPTH, TILE), F32),
            pltpu.VMEM(((tiles + 1) * SUMS, TILE), F32),
            *pairs,
        ],
        compiler_params=params,
    )(positions, incoming, targets, near_acc, items, total)


def solution(mesh):
    in_specs = (
        P(None, "turb", "age"),
        P("turb", "age"),
        P("turb", "age", None, None),
        P("turb", "age", None, None),
        P("turb", "age", None),
        P("turb", "age", None, None),
    )
    out_specs = (P(None, "turb", "age"), P(None, "turb", "age"))
    return jax.shard_map(body, mesh=mesh, in_specs=in_specs, out_specs=out_specs, check_vma=False)
```

```python
import functools

import jax
import jax.numpy as jnp
from jax import lax
from jax.experimental import pallas as pl
from jax.experimental.pallas import tpu as pltpu
from jax.sharding import PartitionSpec as P

SPAN = 64
TILE = 128
time_step = 0.1
core_square = 0.25
inflow_speed = 1.0
inv_four_pi = 0.07957747154594767
GROUP = 8
STEPS = 8
DEPTH = 32
SUMS = 16
F32 = jnp.float32
BF16 = jnp.bfloat16


def split3(value):
    first = value.astype(BF16).astype(F32)
    rest = value - first
    second = rest.astype(BF16).astype(F32)
    third = (rest - second).astype(BF16).astype(F32)
    return first, second, third


def source_rows(middle, strength):
    parts = [split3(-2.0 * middle[comp]) for comp in range(3)]
    square = middle[0] * middle[0] + middle[1] * middle[1] + middle[2] * middle[2] + core_square
    squares = split3(square)
    near_rows = [parts[comp][0] for comp in range(3)] + [parts[comp][1] for comp in range(3)]
    near_rows += [squares[0], squares[1]] + [parts[comp][2] for comp in range(3)] + [squares[2]]
    w1, w2, w = [], [], []
    for comp in range(3):
        first, second, _ = split3(inv_four_pi * strength[comp])
        w1.append(first)
        w2.append(second)
        w.append(first + second)
    u = [
        split3(w[1] * middle[2] - w[2] * middle[1]),
        split3(w[2] * middle[0] - w[0] * middle[2]),
        split3(w[0] * middle[1] - w[1] * middle[0]),
    ]
    strength_rows = w1 + w2 + [u[comp][level] for level in range(3) for comp in range(3)]
    return near_rows, strength_rows


def target_lines(point):
    parts = [split3(point[comp]) for comp in range(3)]
    square = point[0] * point[0] + point[1] * point[1] + point[2] * point[2]
    lines = [(28 + level, row) for level, row in enumerate(split3(square))]
    for comp in range(3):
        first, second, third = parts[comp]
        lines += [(comp, first), (3 + comp, first), (8 + comp, second), (11 + comp, second)]
        lines += [(16 + comp, third), (24 + comp, first)]
    return lines


def fixed_rows(blocks, stage):
    line = lax.broadcasted_iota(jnp.int32, (8, TILE), 0)
    ones = jnp.where((line >= 4) & (line < 7), 1.0, 0.0)

    def fill(b, _):
        stage[pl.ds(pl.multiple_of(b * DEPTH + 8, 8), 8), :] = ones
        stage[pl.ds(pl.multiple_of(b * DEPTH + 24, 8), 8), :] = jnp.zeros_like(ones)
        return 0

    lax.fori_loop(0, blocks, fill, 0, unroll=8)


def pack_sources(blocks, stage, st, ww):
    def pack(b, _):
        base = pl.multiple_of(b * DEPTH, DEPTH)
        top = stage[pl.ds(base, 8), :]
        rest = stage[pl.ds(base + 8, 8), :]
        st[b] = jnp.concatenate([top, top, top, rest], axis=0).astype(BF16).T
        ww[b] = stage[pl.ds(base + 16, SUMS), :].astype(BF16)
        return 0

    lax.fori_loop(0, blocks, pack, 0, unroll=32)


def source_lines(near_rows, strength_rows):
    return list(enumerate(near_rows)) + [(16 + r, row) for r, row in enumerate(strength_rows)]


def left_half(rows):
    return lax.broadcasted_iota(jnp.int32, (rows, TILE), 1) < SPAN


def lattice(here, beyond, circ):
    first = left_half(circ.shape[0])
    middles, strengths = [], []
    for comp in range(3):
        following = jnp.where(first, pltpu.roll(here[comp], SPAN, 1), beyond[comp])
        segment = following - here[comp]
        middles.append(here[comp] + 0.5 * segment)
        strengths.append(circ * segment)
    return middles, strengths


def send_kernel(rows, halves, peers, cap, pos_ref, circ_ref, next_ref, last_ref, list_ref, out_ref, full_ref):
    ends = last_ref[0] == 1
    width = halves * TILE
    for half in range(halves):
        cut = slice(half * TILE, (half + 1) * TILE)
        full_ref[pl.ds(half * 8 + 3, rows, halves * 8), :] = circ_ref[:, cut]
        for comp in range(3):
            full_ref[pl.ds(half * 8 + comp, rows, halves * 8), :] = pos_ref[comp, :, cut]
            if half == halves - 1:
                after = jnp.where(ends, pos_ref[comp, :, width - SPAN :], next_ref[comp])
            else:
                after = pos_ref[comp, :, (half + 1) * TILE : (half + 1) * TILE + SPAN]
            full_ref[pl.ds(half * 8 + 4 + comp, rows, halves * 8), :] = jnp.concatenate([after, after], axis=1)
    first = left_half(3)

    def fill(peer, _):
        base = peer * (cap * 11 // 2)
        after = None
        for c in range(cap):
            block = list_ref[0, c, 0, peer]
            data = full_ref[pl.ds(pl.multiple_of(block * 8, 8), 8), :]
            out_ref[pl.ds(base + c * 4, 4), :] = data[:4]
            if c % 2 == 0:
                after = data[4:7]
            else:
                out_ref[pl.ds(base + cap * 4 + c // 2 * 3, 3), :] = jnp.where(first, after, data[4:7])
        return 0

    lax.fori_loop(0, peers, fill, 0, unroll=2)


def interact(count, item, tt, st, ww, acc, dsc, ksc):
    most = tt.shape[0] - 1

    def distances(step, side):
        for u in range(GROUP):
            target, source = item(step * GROUP + u)
            half = slice((u % 2) * TILE, (u % 2 + 1) * TILE)
            dsc[side, u // 2, :, half] = lax.dot_general(
                st[source], tt[jnp.minimum(target, most)], (((1,), (0,)), ((), ())), preferred_element_type=F32
            )

    def kernels(side):
        for u in range(GROUP // 2):
            inverse = lax.rsqrt(dsc[side, u])
            weight = inverse * inverse * inverse
            high = weight.astype(BF16)
            ksc[side, u, :TILE] = high
            ksc[side, u, TILE:] = (weight - high.astype(F32)).astype(BF16)

    def gather(step, side):
        for u in range(0, GROUP, 2):
            t0, s0 = item(step * GROUP + u)
            t1, s1 = item(step * GROUP + u + 1)
            left = jnp.concatenate([ww[s0], ww[s1]], axis=0)
            left = jnp.concatenate([left, left], axis=1)
            both = lax.dot_general(left, ksc[side, u // 2], (((1,), (0,)), ((), ())), preferred_element_type=F32)
            r0 = pl.ds(pl.multiple_of(t0 * SUMS, SUMS), SUMS)
            acc[r0, :] = acc[r0, :] + both[:SUMS, :TILE]
            r1 = pl.ds(pl.multiple_of(t1 * SUMS, SUMS), SUMS)
            acc[r1, :] = acc[r1, :] + both[SUMS:, TILE:]

    distances(0, 0)
    kernels(0)
    distances(1, 1)

    def turns(first, times, length):
        def turn(index, _):
            for h in range(length):
                step, side = first + index * length + h, h % 2
                gather(step, side)
                kernels(1 - side)
                distances(step + 2, side)
            return 0

        lax.fori_loop(0, times, turn, 0)

    whole = lax.div(count, STEPS // 2)
    turns(0, whole, STEPS)
    turns(whole * STEPS, count - whole * (STEPS // 2), 2)


def near_kernel(
    rows, halves, near, kmax, pos_ref, full_ref, near_ref, slot_ref, count_ref,
    acc_ref, tt_ref, item_ref, total_ref, st, ww, stage, dsc, ksc,
):
    tiles = rows * halves
    line = lax.broadcasted_iota(jnp.int32, (DEPTH, TILE), 0)
    ones = jnp.where((line == 6) | (line == 7) | (line == 27), 1.0, 0.0)

    def blank(b, _):
        stage[pl.ds(pl.multiple_of(b * DEPTH, DEPTH), DEPTH), :] = ones
        return 0

    lax.fori_loop(0, tiles, blank, 0, unroll=8)
    for r, field in target_lines([pos_ref[comp] for comp in range(3)]):
        for half in range(halves):
            stage[pl.ds(half * DEPTH + r, rows, halves * DEPTH), :] = field[:, half * TILE : (half + 1) * TILE]

    def pack(b, _):
        tt_ref[b] = stage[pl.ds(pl.multiple_of(b * DEPTH, DEPTH), DEPTH), :].astype(BF16)
        return 0

    lax.fori_loop(0, tiles, pack, 0, unroll=8)

    def listed(b, at):
        for k in range(kmax):
            item_ref[at + k] = b * 256 + slot_ref[k, b]
        return at + count_ref[b]

    total = lax.fori_loop(0, tiles, listed, 0)
    for k in range(4 * GROUP):
        item_ref[total + k] = tiles * 256
    total_ref[0] = total

    fixed_rows(tiles, stage)
    for half in range(halves):
        parts = [full_ref[pl.ds(half * 8 + line, rows, halves * 8), :] for line in range(7)]
        for r, field in source_lines(*source_rows(*lattice(parts[:3], parts[4:], parts[3]))):
            stage[pl.ds(half * DEPTH + r, rows, halves * DEPTH), :] = field
    pack_sources(tiles, stage, st, ww)
    last = tiles * near - 1

    def item(i):
        i = jnp.minimum(i, last)
        b = lax.div(i, near)
        return b, near_ref[i - b * near, b]

    acc_ref[...] = jnp.zeros_like(acc_ref)
    interact(-(-tiles * near // (2 * GROUP)), item, tt_ref, st, ww, acc_ref, dsc, ksc)


def far_kernel(
    rows, halves, peers, cap, width_rows,
    pos_ref, recv_ref, tt_ref, near_acc, item_ref, total_ref,
    vel_ref, moved_ref,
    st, ww, stage, acc, dsc, ksc,
):
    fixed_rows(peers * cap, stage)

    def lay(group, _):
        for c in range(cap):
            base = group * (8 * width_rows)
            lines = [c * 4 + line for line in range(4)] + [cap * 4 + c // 2 * 3 + comp for comp in range(3)]
            parts = [recv_ref[pl.ds(base + line, 8, width_rows), :] for line in lines]
            beyond = parts[4:] if c % 2 else [pltpu.roll(part, SPAN, 1) for part in parts[4:]]
            for r, field in source_lines(*source_rows(*lattice(parts[:3], beyond, parts[3]))):
                stage[pl.ds(group * (8 * cap * DEPTH) + c * DEPTH + r, 8, cap * DEPTH), :] = field
        return 0

    lax.fori_loop(0, peers // 8, lay, 0, unroll=2)
    pack_sources(peers * cap, stage, st, ww)

    def item(i):
        code = item_ref[i]
        return lax.shift_right_logical(code, 8), lax.bitwise_and(code, 255)

    acc[: rows * halves * SUMS, :] = near_acc[...]
    pairs = lax.div(total_ref[0] + 2 * GROUP - 1, 2 * GROUP)
    interact(pairs, item, tt_ref, st, ww, acc, dsc, ksc)

    for half in range(halves):
        cut = slice(half * TILE, (half + 1) * TILE)

        def summed(*lines):
            value = None
            for line in lines:
                term = acc[pl.ds(half * SUMS + line, rows, halves * SUMS), :]
                value = term if value is None else value + term
            return value

        sums = [summed(3 + comp, comp) for comp in range(3)]
        cross = [summed(12 + comp, 9 + comp, 6 + comp) for comp in range(3)]
        point = [pos_ref[comp, :, cut] for comp in range(3)]
        for comp in range(3):
            j, k = (comp + 1) % 3, (comp + 2) % 3
            velocity = sums[j] * point[k] - sums[k] * point[j] - cross[comp]
            vel_ref[comp, :, cut] = velocity
            inflow = inflow_speed if comp == 0 else 0.0
            moved_ref[comp, :, cut] = point[comp] + time_step * (velocity + inflow)


def body(positions, circulation, send_lists, reader_slots, source_counts, near_blocks):
    _, rows, width = positions.shape
    halves = width // TILE
    tiles = rows * halves
    peers = lax.axis_size("turb")
    cap = send_lists.shape[-1]
    kmax = reader_slots.shape[-1]
    near = near_blocks.shape[-1]
    vmem = pl.BlockSpec(memory_space=pltpu.VMEM)
    smem = pl.BlockSpec(memory_space=pltpu.SMEM)
    ages = lax.axis_size("age")
    next_row = lax.ppermute(positions[:, :, :SPAN], "age", [(s, s - 1) for s in range(1, ages)])
    last = (lax.axis_index("age") == ages - 1).astype(jnp.int32).reshape(1)
    width_rows = cap * 11 // 2
    params = pltpu.CompilerParams(vmem_limit_bytes=48 << 20)

    outgoing, full = pl.pallas_call(
        functools.partial(send_kernel, rows, halves, peers, cap),
        out_shape=(
            jax.ShapeDtypeStruct((peers * width_rows, TILE), F32),
            jax.ShapeDtypeStruct((tiles * 8, TILE), F32),
        ),
        in_specs=[vmem, vmem, vmem, smem, smem],
        out_specs=(vmem, vmem),
        compiler_params=params,
    )(positions, circulation, next_row, last, send_lists.transpose(0, 3, 1, 2))
    incoming = lax.all_to_all(outgoing.reshape(peers, 1, width_rows * TILE), "turb", 0, 0, tiled=True)
    incoming = incoming.reshape(peers * width_rows, TILE)

    pairs = [
        pltpu.VMEM((2, GROUP // 2, TILE, 2 * TILE), F32),
        pltpu.VMEM((2, GROUP // 2, 2 * TILE, 2 * TILE), BF16),
    ]
    near_acc, targets, items, total = pl.pallas_call(
        functools.partial(near_kernel, rows, halves, near, kmax),
        out_shape=(
            jax.ShapeDtypeStruct((tiles * SUMS, TILE), F32),
            jax.ShapeDtypeStruct((tiles, DEPTH, TILE), BF16),
            jax.ShapeDtypeStruct((tiles * kmax + 64,), jnp.int32),
            jax.ShapeDtypeStruct((1,), jnp.int32),
        ),
        in_specs=[vmem, vmem, smem, smem, smem],
        out_specs=(vmem, vmem, smem, smem),
        scratch_shapes=[
            pltpu.VMEM((tiles, TILE, DEPTH), BF16),
            pltpu.VMEM((tiles, SUMS, TILE), BF16),
            pltpu.VMEM((tiles * DEPTH, TILE), F32),
            *pairs,
        ],
        compiler_params=params,
        cost_estimate=pl.CostEstimate(flops=2 * 10**9, bytes_accessed=4 << 20, transcendentals=tiles * near * TILE * TILE),
    )(positions, full, near_blocks[0, 0].T, reader_slots[0, 0].T, source_counts[0, 0])
    return pl.pallas_call(
        functools.partial(far_kernel, rows, halves, peers, cap, width_rows),
        out_shape=(
            jax.ShapeDtypeStruct(positions.shape, F32),
            jax.ShapeDtypeStruct(positions.shape, F32),
        ),
        in_specs=[vmem, vmem, vmem, vmem, smem, smem],
        out_specs=(vmem, vmem),
        scratch_shapes=[
            pltpu.VMEM((peers * cap, TILE, DEPTH), BF16),
            pltpu.VMEM((peers * cap, SUMS, TILE), BF16),
            pltpu.VMEM((peers * cap * DEPTH, TILE), F32),
            pltpu.VMEM(((tiles + 1) * SUMS, TILE), F32),
            *pairs,
        ],
        compiler_params=params,
    )(positions, incoming, targets, near_acc, items, total)


def solution(mesh):
    in_specs = (
        P(None, "turb", "age"),
        P("turb", "age"),
        P("turb", "age", None, None),
        P("turb", "age", None, None),
        P("turb", "age", None),
        P("turb", "age", None, None),
    )
    out_specs = (P(None, "turb", "age"), P(None, "turb", "age"))
    return jax.shard_map(body, mesh=mesh, in_specs=in_specs, out_specs=out_specs, check_vma=False)
```
